256 devices in a mesh: fsdp: 64 (over y, z, core), tp: 4 (over x).
Axes of the slice: x: 4, y: 4, z: 8, core: 2. Of those that a mesh axis runs over, the one named last changes fastest.
Arguments:
- momentum: float32 [18432, 7168], P('fsdp', 'tp'), may hold values from -120 to 120
- gradient: bfloat16 [18432, 7168], P('fsdp', 'tp'), may hold values from -4 to 4
- column_basis: bfloat16 [7168, 896], P('tp'), may hold values from -0.0625 to 0.0625
Outputs:
- momentum_new: float32 [18432, 7168], P('fsdp', 'tp')
- update: bfloat16 [18432, 7168], P('fsdp', 'tp')
- new_basis: bfloat16 [7168, 896], P('tp')
The draws below stay inside these ranges and needn't reach their ends.
All inputs are finite; a program needn't handle non-finite values.
Results may differ from the reference program's by a relative error of at most 0.007.
Values may be sent and summed in bfloat16 or wider, within the bound.
A program may use at most 128 MiB of HBM per device.

```python
import math
import jax
import jax.numpy as jnp
from jax import lax

ROWS_FF = 18432
COLS_D = 7168
RANK = 896


def draw_momentum(key, part):
    key = jax.random.fold_in(key, 11)
    key_rows, key_cols, key_base = jax.random.split(key, 3)
    row_ramp = 0.6 + 1.2 * jnp.arange(ROWS_FF, dtype=jnp.float32)[:, None] / ROWS_FF
    col_ramp = 0.6 + 1.2 * jnp.arange(COLS_D, dtype=jnp.float32)[None, :] / COLS_D
    scale_low = 0.25
    scale_high = 2.5
    base_values = jnp.clip(jax.random.normal(key_base, (ROWS_FF, COLS_D), jnp.float32), -5.0, 5.0)
    row_scale = jnp.exp(jax.random.uniform(key_rows, (ROWS_FF, 1), jnp.float32, math.log(scale_low), math.log(scale_high))) * row_ramp
    col_scale = jnp.exp(jax.random.uniform(key_cols, (1, COLS_D), jnp.float32, math.log(scale_low), math.log(scale_high))) * col_ramp
    return (row_scale * col_scale * base_values).astype(jnp.float32)


def shard_levels(own_key, dims, cuts, smallest, top_value):
    def one(position, blocks):
        steps = jax.random.uniform(jax.random.fold_in(jax.random.fold_in(own_key, 6), position), (blocks,), jnp.float32, smallest / len(cuts), top_value / len(cuts))
        return jnp.repeat(jnp.exp(steps), dims[position] // blocks).reshape((-1,) + (1,) * (len(dims) - position - 1))

    level = one(*cuts[0])
    for cut in cuts[1:]:
        level = level * one(*cut)
    return level


def noise(own_key, extent, width, most, pieces=(), kind=jnp.bfloat16):
    level = shard_levels(own_key, extent, pieces, -0.22, 0.18) if pieces else 1.0
    values = jax.random.normal(own_key, extent, jnp.float32) * width * level
    return jnp.minimum(jnp.maximum(values, -most), most).astype(kind)


def setup_inputs(seed: int = 0) -> dict:
    streams_of = jax.random.split(jax.random.key(seed), 4)
    return {
        "momentum": draw_momentum(jax.random.fold_in(streams_of[3], 71), 0),
        "gradient": noise(streams_of[1], (ROWS_FF, COLS_D), 0.5, 4.0, ((0, 64), (1, 4))),
        "column_basis": noise(streams_of[2], (COLS_D, RANK), COLS_D ** -0.5, 0.0625, ((0, 4),)),
    }


RIDGE = 0.001
DECAY = 0.8
EPS = 1e-06

def reference(momentum, gradient, column_basis):
    blended = momentum + gradient.astype(jnp.float32)
    blended_low = blended.astype(jnp.bfloat16)
    projected = jnp.dot(blended_low.astype(jnp.float32), column_basis.astype(jnp.float32), preferred_element_type=jnp.float32)
    gram_matrix = lax.dot_general(projected.astype(jnp.float32), projected.astype(jnp.float32), (((0,), (0,)), ((), ())), precision=lax.Precision.HIGHEST, preferred_element_type=jnp.float32)
    gram_matrix = gram_matrix + RIDGE * jnp.eye(RANK, dtype=jnp.float32)
    lower_factor = jnp.linalg.cholesky(gram_matrix)
    orthonormal = lax.linalg.triangular_solve(lower_factor, projected, left_side=False, lower=True, transpose_a=True)
    ortho_low = orthonormal.astype(jnp.bfloat16)
    right_factor = lax.dot_general(blended_low.astype(jnp.float32), ortho_low.astype(jnp.float32), (((0,), (0,)), ((), ())), preferred_element_type=jnp.float32)
    column_rms = jnp.sqrt(lax.optimization_barrier(jnp.sum(right_factor * right_factor, axis=0)) / COLS_D + EPS)
    new_basis = (right_factor / column_rms).astype(jnp.bfloat16)
    feed_low = (orthonormal * column_rms).astype(jnp.bfloat16)
    feedback = lax.dot_general(feed_low.astype(jnp.float32), new_basis.astype(jnp.float32), (((1,), (1,)), ((), ())), preferred_element_type=jnp.float32)
    momentum_new = blended - (1.0 - DECAY) * feedback
    direction = lax.dot_general(ortho_low.astype(jnp.float32), new_basis.astype(jnp.float32), (((1,), (1,)), ((), ())), preferred_element_type=jnp.float32)
    update = (math.sqrt(ROWS_FF / RANK) * direction).astype(jnp.bfloat16)
    return (momentum_new, update, new_basis)
```

```python
import math

import jax
import jax.numpy as jnp
from jax import lax
from jax.experimental import pallas as pl
from jax.experimental.pallas import tpu as pltpu
from jax.sharding import PartitionSpec as P

ROWS_FF = 18432
COLS_D = 7168
RANK = 896

RIDGE = 0.001
DECAY = 0.8
EPS = 1e-06
HI = lax.Precision.HIGHEST
F32 = jnp.float32
BF16 = jnp.bfloat16
NB = 128
NBLK = RANK // NB
MESH = pl.DeviceIdType.MESH
NX, NY, NZ = 4, 4, 8


class Links:
    def __init__(self):
        f = lax.axis_index("fsdp")
        self.x = lax.axis_index("tp")
        self.core = lax.rem(f, 2)
        self.z = lax.rem(f // 2, NZ)
        self.y = f // (2 * NZ)

    def at_x(self, d):
        t = lax.rem(self.x + d, NX)
        return t, {"tp": t}

    def at_y(self, d):
        t = lax.rem(self.y + d, NY)
        return t, {"fsdp": (t * NZ + self.z) * 2 + self.core}

    def at_z(self, d):
        t = lax.rem(self.z + d, NZ)
        return t, {"fsdp": (self.y * NZ + t) * 2 + self.core}

    def at_zc(self, d):
        t = lax.rem(self.z * 2 + self.core + d, 2 * NZ)
        return t, {"fsdp": self.y * NZ * 2 + t}

    def at_xy(self, dx, dy):
        tx, ty = lax.rem(self.x + dx, NX), lax.rem(self.y + dy, NY)
        return tx * NY + ty, {"tp": tx, "fsdp": (ty * NZ + self.z) * 2 + self.core}

    def at_core(self):
        t = 1 - self.core
        return t, {"fsdp": (self.y * NZ + self.z) * 2 + t}


class Copies:
    def __init__(self, send_sems, recv_sems):
        self.send_sems, self.recv_sems = send_sems, recv_sems
        self.count = 0
        self.started = []

    def start(self, src, dst, device, when=None):
        copy = pltpu.make_async_remote_copy(
            src_ref=src, dst_ref=dst, send_sem=self.send_sems.at[self.count],
            recv_sem=self.recv_sems.at[self.count], device_id=device, device_id_type=MESH)
        self.count += 1
        if when is None:
            copy.start()
        else:
            pl.when(when)(copy.start)
        self.started.append((copy, when))
        return copy

    def finish(self):
        for copy, when in self.started:
            if when is None:
                copy.wait_send()
            else:
                pl.when(when)(copy.wait_send)
        self.started = []


def greet(links, along):
    barrier = pltpu.get_barrier_semaphore()
    partners = []
    if "x" in along:
        partners += [links.at_x(d)[1] for d in range(1, NX)]
    if "y" in along:
        partners += [links.at_y(d)[1] for d in range(1, NY)]
    if "z" in along:
        partners += [links.at_z(d)[1] for d in range(1, NZ)]
    if "c" in along:
        partners += [links.at_core()[1]]
    if "Z" in along:
        partners += [links.at_zc(d)[1] for d in range(1, 2 * NZ)]
    if "X" in along:
        partners += [links.at_xy(dx, dy)[1] for dx in range(NX) for dy in range(NY) if dx or dy]
    for device in partners:
        pl.semaphore_signal(barrier, inc=1, device_id=device, device_id_type=MESH)
    return barrier, len(partners)


def rows(start, size):
    return pl.ds(pl.multiple_of(start, 8), size)


GRAM_COPIES = 3 + 1 + 6 + 6 + 7 + 3 + 6 + 6 + 1 + 1


def cross_half(low, projected, half):
    lhs = low[:, pl.ds(pl.multiple_of(half * RANK, NB), RANK)]
    p = projected[...]
    high = p.astype(BF16)
    rest = (p - high.astype(F32)).astype(BF16)
    dims = (((0,), (0,)), ((), ()))
    return (lax.dot_general(lhs, high, dims, preferred_element_type=F32)
            + lax.dot_general(lhs, rest, dims, preferred_element_type=F32))


def gram_kernel(mom, grad, basis, p_out, g_out, s_out, pp, prx, pc, pf, ga, r1, s1, r2, zr, a4, gf, low, so, sr, ssem, rsem):
    lk = Links()
    cp = Copies(ssem, rsem)
    barrier, partners = greet(lk, "xyzc")
    part = pp.shape[0] // NX
    step = 96
    for c in range(pp.shape[0] // step):
        at = pl.ds(c * step, step)
        low[at, :] = (mom[at, :] + grad[at, :].astype(F32)).astype(BF16)
        pp[at, :] = jnp.dot(low[at, :], basis[...], preferred_element_type=F32)
    pl.semaphore_wait(barrier, partners)
    sent = []
    for d in range(1, NX):
        t, dev = lk.at_x(d)
        sent.append(cp.start(pp.at[rows(t * part, part)], prx.at[d - 1], dev))
    for copy in sent:
        copy.wait_recv()
    mine = pp[rows(lk.x * part, part), :] + prx[0] + prx[1] + prx[2]
    pf[rows(lk.x * part, part), :] = mine
    pc[rows(lk.core * part, part), pl.ds(0, RANK)] = mine
    half = pc.at[rows(lk.core * part, part), pl.ds(0, RANK)]
    copy = cp.start(half, half, lk.at_core()[1])
    copy.wait_recv()
    pc[:, pl.ds(RANK, 3 * NB)] = pc[:, pl.ds(0, 3 * NB)]
    for b in range(NBLK):
        blocks = lax.dot_general(
            pc[:, pl.ds(b * NB, NB)],
            pc[:, pl.ds(pl.multiple_of((b + 2 * lk.core) * NB, NB), 2 * NB)],
            (((0,), (0,)), ((), ())), precision=HI, preferred_element_type=F32)
        ga[0, pl.ds(b * NB, NB), :] = blocks[:, :NB]
        ga[1, pl.ds(b * NB, NB), :] = blocks[:, NB:]
    big, small = RANK // 4, RANK // 16
    sent = []
    for d in range(1, 4):
        tx, dx = lk.at_x(d)
        ty, dy = lk.at_y(d)
        sent.append(cp.start(ga.at[0, rows(tx * big, big)], r1.at[0, d - 1], dx))
        sent.append(cp.start(ga.at[1, rows(ty * big, big)], r1.at[1, d - 1], dy))
    for copy in sent:
        copy.wait_recv()
    s1[0] = ga[0, rows(lk.x * big, big), :] + r1[0, 0] + r1[0, 1] + r1[0, 2]
    s1[1] = ga[1, rows(lk.y * big, big), :] + r1[1, 0] + r1[1, 1] + r1[1, 2]
    sent = []
    for d in range(1, 4):
        tx, dx = lk.at_x(d)
        ty, dy = lk.at_y(d)
        sent.append(cp.start(s1.at[0, rows(ty * small, small)], r2.at[0, d - 1], dy))
        sent.append(cp.start(s1.at[1, rows(tx * small, small)], r2.at[1, d - 1], dx))
    for copy in sent:
        copy.wait_recv()
    zr[lk.z, pl.ds(0, small), :] = s1[0, rows(lk.y * small, small), :] + r2[0, 0] + r2[0, 1] + r2[0, 2]
    zr[lk.z, pl.ds(small, small), :] = s1[1, rows(lk.x * small, small), :] + r2[1, 0] + r2[1, 1] + r2[1, 2]
    sent = []
    for d in range(1, NZ):
        sent.append(cp.start(zr.at[lk.z], zr.at[lk.z], lk.at_z(d)[1]))
    rest = []
    own_rows = pf.at[rows(lk.x * part, part)]
    for d in range(1, NX):
        rest.append(cp.start(own_rows, own_rows, lk.at_x(d)[1]))
    for copy in sent:
        copy.wait_recv()
    total = zr[0]
    for i in range(1, NZ):
        total = total + zr[i]
    a4[0, rows(lk.y * small, small), :] = total[:small]
    a4[1, rows(lk.x * small, small), :] = total[small:]
    sent = []
    for d in range(1, 4):
        own0 = a4.at[0, rows(lk.y * small, small)]
        own1 = a4.at[1, rows(lk.x * small, small)]
        sent.append(cp.start(own0, own0, lk.at_y(d)[1]))
        sent.append(cp.start(own1, own1, lk.at_x(d)[1]))
    for copy in rest:
        copy.wait_recv()
    so[...] = cross_half(low, pf, 1 - lk.core)
    cross = cp.start(so, sr, lk.at_core()[1])
    for copy in sent:
        copy.wait_recv()
    gf[lk.core, 0, rows(lk.x * big, big), :] = a4[0]
    gf[lk.core, 1, rows(lk.y * big, big), :] = a4[1]
    sent = []
    for d in range(1, 4):
        own0 = gf.at[lk.core, 0, rows(lk.x * big, big)]
        own1 = gf.at[lk.core, 1, rows(lk.y * big, big)]
        sent.append(cp.start(own0, own0, lk.at_x(d)[1]))
        sent.append(cp.start(own1, own1, lk.at_y(d)[1]))
    s_out[...] = cross_half(low, pf, lk.core)
    for copy in sent:
        copy.wait_recv()
    copy = cp.start(gf.at[lk.core], gf.at[lk.core], lk.at_core()[1])
    cross.wait_recv()
    s_out[...] += sr[...]
    copy.wait_recv()
    cp.finish()
    p_out[...] = pf[...]
    g_out[...] = gf[...]


def project_and_gram(momentum, gradient, basis):
    n, big, small = momentum.shape[0], RANK // 4, RANK // 16
    vm = pl.BlockSpec(memory_space=pltpu.VMEM)
    return pl.pallas_call(
        gram_kernel,
        out_shape=(jax.ShapeDtypeStruct((n, RANK), F32), jax.ShapeDtypeStruct((2, 2, RANK, NB), F32),
                   jax.ShapeDtypeStruct((RANK, RANK), F32)),
        in_specs=[vm] * 3,
        out_specs=(vm,) * 3,
        scratch_shapes=[
            pltpu.VMEM((n, RANK), F32),
            pltpu.VMEM((3, n // NX, RANK), F32),
            pltpu.VMEM((2 * n // NX, RANK + 3 * NB), F32),
            pltpu.VMEM((n, RANK), F32),
            pltpu.VMEM((2, RANK, NB), F32),
            pltpu.VMEM((2, 3, big, NB), F32),
            pltpu.VMEM((2, big, NB), F32),
            pltpu.VMEM((2, 3, small, NB), F32),
            pltpu.VMEM((NZ, 2 * small, NB), F32),
            pltpu.VMEM((2, big, NB), F32),
            pltpu.VMEM((2, 2, RANK, NB), F32),
            pltpu.VMEM(momentum.shape, BF16),
            pltpu.VMEM((RANK, RANK), F32),
            pltpu.VMEM((RANK, RANK), F32),
            pltpu.SemaphoreType.DMA((GRAM_COPIES,)),
            pltpu.SemaphoreType.DMA((GRAM_COPIES,)),
        ],
        compiler_params=pltpu.CompilerParams(
            collective_id=0, has_side_effects=True, vmem_limit_bytes=48 * 2**20),
    )(momentum, gradient, basis)


def factor128(T):
    lane = lax.broadcasted_iota(jnp.int32, (8, 128), 1)
    sub = lax.broadcasted_iota(jnp.int32, (8, 128), 0)
    T = list(T)
    out = []
    for s in range(16):
        V = T[s]
        def lb(x, c):
            return jnp.broadcast_to(x[:, c:c + 1], (8, 128))
        def sb(x, r):
            return jnp.broadcast_to(x[r:r + 1, :], (8, 128))
        E = [lb(V, 8 * s + c) for c in range(8)]
        a = {}
        for c in range(8):
            for r in range(c, 8):
                a[r, c] = sb(E[c], r)
        inblk = (lane >= 8 * s) & (lane < 8 * s + 8)
        Vp = jnp.where(inblk, jnp.where(lane - 8 * s == sub, 1.0, 0.0), V)
        y = [sb(Vp, r) for r in range(8)]
        rp = [None] * 8
        d = [None] * 8
        l = {}
        for j in range(8):
            d[j] = a[j, j]
            rp[j] = pl.reciprocal(d[j], approx=False)
            for i in range(j + 1, 8):
                l[i, j] = a[i, j] * rp[j]
            for i in range(j + 1, 8):
                for k in range(j + 1, i + 1):
                    a[i, k] = a[i, k] - l[i, j] * a[k, j]
            for i in range(j + 1, 8):
                y[i] = y[i] - l[i, j] * y[j]
        z = [y[j] * rp[j] for j in range(8)]
        R = y[0] * lax.rsqrt(d[0])
        for j in range(1, 8):
            R = jnp.where(sub == j, y[j] * lax.rsqrt(d[j]), R)
        out.append(jnp.where(lane < 8 * s + 8, R, 0.0))
        if s < 15:
            q = [None] * 8
            for j in range(7, -1, -1):
                acc = z[j]
                for i in range(j + 1, 8):
                    acc = acc - l[i, j] * q[i]
                q[j] = acc
            for t in range(s + 1, 16):
                Et = [lb(T[t], 8 * s + c) for c in range(8)]
                base = jnp.where(inblk, 0.0, T[t])
                if t == s + 1:
                    for j in range(8):
                        for i in range(j + 1, 8):
                            Et[i] = Et[i] - l[i, j] * Et[j]
                    acc = base
                    for j in range(8):
                        acc = acc - Et[j] * z[j]
                else:
                    acc = base
                    for j in range(8):
                        acc = acc - Et[j] * q[j]
                T[t] = acc
    return out


def assemble(g_ref, w):
    eye = jnp.where(
        lax.broadcasted_iota(jnp.int32, (NB, NB), 0) == lax.broadcasted_iota(jnp.int32, (NB, NB), 1), RIDGE, 0.0)
    for d in range(4):
        for b in range(NBLK):
            c = (b + d) % NBLK
            block = g_ref[d // 2, d % 2, b * NB:(b + 1) * NB, :]
            if d == 0:
                block = block + eye
            if b <= c:
                w[b * NB:(b + 1) * NB, c * NB:(c + 1) * NB] = block
            else:
                w[c * NB:(c + 1) * NB, b * NB:(b + 1) * NB] = block.T


def factor_step(w, k):
    o = pl.multiple_of(k * NB, NB)
    tiles = [w[pl.ds(pl.multiple_of(o + 8 * t, 8), 8), pl.ds(o, NB)] for t in range(16)]
    diag = jnp.concatenate(factor128(tiles), axis=0)
    w[pl.ds(o, NB), :] = jnp.dot(diag, w[pl.ds(o, NB), :], precision=HI, preferred_element_type=F32)
    w[pl.ds(o, NB), pl.ds(o, NB)] = diag

    def update(i, _):
        r = pl.multiple_of(i * NB, NB)
        upper = w[pl.ds(o, NB), pl.ds(r, NB)]
        w[pl.ds(r, NB), pl.ds(o, NB)] = jnp.zeros((NB, NB), F32)
        w[pl.ds(r, NB), :] -= lax.dot_general(
            upper, w[pl.ds(o, NB), :], (((0,), (0,)), ((), ())), precision=HI, preferred_element_type=F32)
        return 0

    lax.fori_loop(k + 1, NBLK, update, 0)


def times_inverse(left, w, k):
    n = (k + 1) * NB
    return lax.dot_general(
        left[:, :n], w[k * NB:n, :n], (((1,), (1,)), ((), ())), precision=HI, preferred_element_type=F32)


OWN = 7
FACTOR_COPIES = 3 + 7 + 7 + 3 + 15 + 15 + 7 + 3 + 3 + 7 + 1


def factor_kernel(g_ref, s_ref, p_ref, nb_out, low_out, w, ra1, rb1, sa, sb, ra2, rb2, rf, sq1, sq2, nb, ssem, rsem):
    lk = Links()
    cp = Copies(ssem, rsem)
    barrier, partners = greet(lk, "ZX")
    owner = lk.z < OWN
    zc = jnp.minimum(lk.z, OWN - 1)
    assemble(g_ref, w)
    pl.semaphore_wait(barrier, partners)
    half = RANK // 2
    ya, za, piece = half // NY, half // OWN, half // NY // OWN
    first_a, first_b = [], []
    for d in range(1, NY):
        t, dev = lk.at_y(d)
        first_a.append(cp.start(s_ref.at[rows(t * ya, ya)], ra1.at[d - 1], dev))
    for d in range(1, NZ):
        t, dev = lk.at_z(d)
        src = s_ref.at[rows(half + jnp.minimum(t, OWN - 1) * za, za)]
        first_b.append(cp.start(src, rb1.at[d - 1], dev, when=t < OWN))
    lax.fori_loop(0, 3, lambda k, _: (factor_step(w, k), 0)[1], 0)
    for copy in first_a:
        copy.wait_recv()
    sa[...] = s_ref[rows(lk.y * ya, ya), :] + ra1[0] + ra1[1] + ra1[2]
    second_a, second_b = [], []
    for d in range(1, NZ):
        t, dev = lk.at_z(d)
        src = sa.at[rows(jnp.minimum(t, OWN - 1) * piece, piece)]
        second_a.append(cp.start(src, ra2.at[d - 1], dev, when=t < OWN))
    lax.fori_loop(3, 6, lambda k, _: (factor_step(w, k), 0)[1], 0)

    @pl.when(owner)
    def _():
        for copy in first_b:
            copy.wait_recv()
        total = s_ref[rows(half + zc * za, za), :]
        for i in range(OWN):
            total = total + rb1[i]
        sb[...] = total

    for d in range(1, NY):
        t, dev = lk.at_y(d)
        second_b.append(cp.start(sb.at[rows(t * piece, piece)], rb2.at[d - 1], dev, when=owner))
    lax.fori_loop(6, NBLK, lambda k, _: (factor_step(w, k), 0)[1], 0)

    @pl.when(owner)
    def _():
        for copy in second_a:
            copy.wait_recv()
        total = sa[rows(zc * piece, piece), :]
        for i in range(OWN):
            total = total + ra2[i]
        rf[0:piece, :] = total
        for copy in second_b:
            copy.wait_recv()
        rf[piece:2 * piece, :] = sb[rows(lk.y * piece, piece), :] + rb2[0] + rb2[1] + rb2[2]

    @pl.when(jnp.logical_not(owner))
    def _():
        rf[...] = jnp.zeros_like(rf)

    left = rf[...]
    right = [times_inverse(left, w, k) for k in range(NBLK)]
    me1 = lk.z * 2 + lk.core
    me2 = lk.x * NY + lk.y
    for k in range(NBLK):
        sq1[me1, k:k + 1, :] = jnp.sum(right[k] * right[k], axis=0, keepdims=True)
    sq1[me1, NBLK:, :] = jnp.zeros((1, NB), F32)
    sent = [cp.start(sq1.at[me1], sq1.at[me1], lk.at_zc(d)[1]) for d in range(1, 2 * NZ)]
    for copy in sent:
        copy.wait_recv()
    total = sq1[0]
    for i in range(1, 2 * NZ):
        total = total + sq1[i]
    sq2[me2] = total
    sent = [cp.start(sq2.at[me2], sq2.at[me2], lk.at_xy(dx, dy)[1])
            for dx in range(NX) for dy in range(NY) if dx or dy]
    for copy in sent:
        copy.wait_recv()
    total = sq2[0]
    for i in range(1, NX * NY):
        total = total + sq2[i]
    rms = jnp.sqrt(total / COLS_D + EPS)
    base = lk.core * RANK
    for k in range(NBLK):
        at = slice(k * NB, (k + 1) * NB)
        normal = (right[k] / rms[k:k + 1, :]).astype(BF16)

        @pl.when(owner)
        def _():
            nb[rows16(base + lk.y * ya + zc * piece, piece), at] = normal[:piece]
            nb[rows16(base + half + zc * za + lk.y * piece, piece), at] = normal[piece:]

    ga, gb = [], []
    own_a = nb.at[rows16(base + lk.y * ya + zc * piece, piece)]
    own_b = nb.at[rows16(base + half + zc * za + lk.y * piece, piece)]
    for d in range(1, NY):
        gb.append(cp.start(own_b, own_b, lk.at_y(d)[1], when=owner))
    for d in range(1, NZ):
        ga.append(cp.start(own_a, own_a, lk.at_z(d)[1], when=owner))

    @pl.when(owner)
    def _():
        for copy in gb:
            copy.wait_recv()

    gb = []
    own_b = nb.at[rows16(base + half + zc * za, za)]
    for d in range(1, NZ):
        gb.append(cp.start(own_b, own_b, lk.at_z(d)[1], when=owner))
    for d in range(1, NZ):
        pl.when(lax.rem(lk.z + NZ - d, NZ) < OWN)(ga[d - 1].wait_recv)
    ga = []
    own_a = nb.at[rows16(base + lk.y * ya, ya)]
    for d in range(1, NY):
        ga.append(cp.start(own_a, own_a, lk.at_y(d)[1]))
    left = p_ref[...]
    n = p_ref.shape[0]
    for k in range(NBLK):
        at = slice(k * NB, (k + 1) * NB)
        ortho = times_inverse(left, w, k)
        low_out[:n, at] = (ortho * rms[k:k + 1, :]).astype(BF16)
        low_out[n:, at] = ortho.astype(BF16)
    for copy in ga:
        copy.wait_recv()
    for d in range(1, NZ):
        pl.when(lax.rem(lk.z + NZ - d, NZ) < OWN)(gb[d - 1].wait_recv)
    own = nb.at[rows16(base, RANK)]
    copy = cp.start(own, own, lk.at_core()[1])
    copy.wait_recv()
    cp.finish()
    nb_out[...] = nb[...]


def rows16(start, size):
    return pl.ds(pl.multiple_of(start, 16), size)


def factor_and_basis(gram, cross, projected):
    n = projected.shape[0]
    vm = pl.BlockSpec(memory_space=pltpu.VMEM)
    half = RANK // 2
    ya, za, piece = half // NY, half // OWN, half // NY // OWN
    return pl.pallas_call(
        factor_kernel,
        out_shape=(jax.ShapeDtypeStruct((2 * RANK, RANK), BF16), jax.ShapeDtypeStruct((2 * n, RANK), BF16)),
        in_specs=[vm] * 3,
        out_specs=(vm, vm),
        scratch_shapes=[
            pltpu.VMEM((RANK, RANK), F32),
            pltpu.VMEM((NY - 1, ya, RANK), F32),
            pltpu.VMEM((NZ - 1, za, RANK), F32),
            pltpu.VMEM((ya, RANK), F32),
            pltpu.VMEM((za, RANK), F32),
            pltpu.VMEM((NZ - 1, piece, RANK), F32),
            pltpu.VMEM((NY - 1, piece, RANK), F32),
            pltpu.VMEM((2 * piece, RANK), F32),
            pltpu.VMEM((2 * NZ, 8, NB), F32),
            pltpu.VMEM((NX * NY, 8, NB), F32),
            pltpu.VMEM((2 * RANK, RANK), BF16),
            pltpu.SemaphoreType.DMA((FACTOR_COPIES,)),
            pltpu.SemaphoreType.DMA((FACTOR_COPIES,)),
        ],
        compiler_params=pltpu.CompilerParams(
            collective_id=1, has_side_effects=True, vmem_limit_bytes=48 * 2**20),
    )(gram, cross, projected)


def body(momentum, gradient, column_basis):
    projected, gram, cross = project_and_gram(momentum, gradient, column_basis)
    new_basis, stacked = factor_and_basis(gram, cross, projected)
    blended = momentum + gradient.astype(F32)
    products = lax.dot_general(
        stacked, new_basis, (((1,), (1,)), ((), ())), preferred_element_type=F32
    )
    rows_here = momentum.shape[0]
    momentum_new = blended - (1.0 - DECAY) * products[:rows_here]
    update = (math.sqrt(ROWS_FF / RANK) * products[rows_here:]).astype(BF16)
    return (momentum_new, update, new_basis)


def solution(mesh):
    placed = (P("fsdp", "tp"), P("fsdp", "tp"), P("tp", None))
    return jax.shard_map(
        body,
        mesh=mesh,
        in_specs=placed,
        out_specs=(P("fsdp", "tp"), P("fsdp", "tp"), P("tp", None)),
        check_vma=False,
    )
```

```python
import math

import jax
import jax.numpy as jnp
from jax import lax
from jax.experimental import pallas as pl
from jax.experimental.pallas import tpu as pltpu
from jax.sharding import PartitionSpec as P

ROWS_FF = 18432
COLS_D = 7168
RANK = 896

RIDGE = 0.001
DECAY = 0.8
EPS = 1e-06
HI = lax.Precision.HIGHEST
F32 = jnp.float32
BF16 = jnp.bfloat16
NB = 128
NBLK = RANK // NB
MESH = pl.DeviceIdType.MESH
NX, NY, NZ = 4, 4, 8


class Links:
    def __init__(self):
        f = lax.axis_index("fsdp")
        self.x = lax.axis_index("tp")
        self.core = lax.rem(f, 2)
        self.z = lax.rem(f // 2, NZ)
        self.y = f // (2 * NZ)

    def at_x(self, d):
        t = lax.rem(self.x + d, NX)
        return t, {"tp": t}

    def at_y(self, d):
        t = lax.rem(self.y + d, NY)
        return t, {"fsdp": (t * NZ + self.z) * 2 + self.core}

    def at_z(self, d):
        t = lax.rem(self.z + d, NZ)
        return t, {"fsdp": (self.y * NZ + t) * 2 + self.core}

    def at_zc(self, d):
        t = lax.rem(self.z * 2 + self.core + d, 2 * NZ)
        return t, {"fsdp": self.y * NZ * 2 + t}

    def at_xy(self, dx, dy):
        tx, ty = lax.rem(self.x + dx, NX), lax.rem(self.y + dy, NY)
        return tx * NY + ty, {"tp": tx, "fsdp": (ty * NZ + self.z) * 2 + self.core}

    def at_core(self):
        t = 1 - self.core
        return t, {"fsdp": (self.y * NZ + self.z) * 2 + t}


class Copies:
    def __init__(self, send_sems, recv_sems):
        self.send_sems, self.recv_sems = send_sems, recv_sems
        self.count = 0
        self.started = []

    def make(self, src, dst, device, when=None, slot=None):
        arrival = self.count if slot is None else slot
        copy = pltpu.make_async_remote_copy(
            src_ref=src, dst_ref=dst, send_sem=self.send_sems.at[self.count],
            recv_sem=self.recv_sems.at[arrival], device_id=device, device_id_type=MESH)
        self.count += 1
        self.started.append((copy, when))
        return copy

    def start(self, src, dst, device, when=None, slot=None):
        copy = self.make(src, dst, device, when, slot)
        if when is None:
            copy.start()
        else:
            pl.when(when)(copy.start)
        return copy

    def finish(self):
        for copy, when in self.started:
            if when is None:
                copy.wait_send()
            else:
                pl.when(when)(copy.wait_send)
        self.started = []


def greet(links, along):
    barrier = pltpu.get_barrier_semaphore()
    partners = []
    if "x" in along:
        partners += [links.at_x(d)[1] for d in range(1, NX)]
    if "y" in along:
        partners += [links.at_y(d)[1] for d in range(1, NY)]
    if "z" in along:
        partners += [links.at_z(d)[1] for d in range(1, NZ)]
    if "c" in along:
        partners += [links.at_core()[1]]
    if "Z" in along:
        partners += [links.at_zc(d)[1] for d in range(1, 2 * NZ)]
    if "X" in along:
        partners += [links.at_xy(dx, dy)[1] for dx in range(NX) for dy in range(NY) if dx or dy]
    for device in partners:
        pl.semaphore_signal(barrier, inc=1, device_id=device, device_id_type=MESH)
    return barrier, len(partners)


def rows(start, size):
    return pl.ds(pl.multiple_of(start, 8), size)


def cross_half(low, projected, half):
    lhs = low[:, pl.ds(pl.multiple_of(half * RANK, NB), RANK)]
    p = projected[...]
    high = p.astype(BF16)
    rest = (p - high.astype(F32)).astype(BF16)
    dims = (((0,), (0,)), ((), ()))
    return (lax.dot_general(lhs, high, dims, preferred_element_type=F32)
            + lax.dot_general(lhs, rest, dims, preferred_element_type=F32))


def factor128(tiles):
    lane = lax.broadcasted_iota(jnp.int32, (8, 128), 1)
    sub = lax.broadcasted_iota(jnp.int32, (8, 128), 0)
    tiles = list(tiles)
    out = []

    def over_lanes(x, c):
        return jnp.broadcast_to(x[:, c:c + 1], (8, 128))

    def over_rows(x, r):
        return jnp.broadcast_to(x[r:r + 1, :], (8, 128))

    diag = [over_lanes(tiles[0], c) for c in range(8)]
    for s in range(16):
        a = {(r, c): over_rows(diag[c], r) for c in range(8) for r in range(c, 8)}
        inside = (lane >= 8 * s) & (lane < 8 * s + 8)
        row = jnp.where(inside, jnp.where(lane - 8 * s == sub, 1.0, 0.0), tiles[s])
        y = [over_rows(row, r) for r in range(8)]
        inv, low = [None] * 8, {}
        for j in range(8):
            inv[j] = pl.reciprocal(a[j, j], approx=False)
            for i in range(j + 1, 8):
                low[i, j] = a[i, j] * inv[j]
            for i in range(j + 1, 8):
                for k in range(j + 1, i + 1):
                    a[i, k] = a[i, k] - low[i, j] * a[k, j]
            for i in range(j + 1, 8):
                y[i] = y[i] - low[i, j] * y[j]
        z = [y[j] * inv[j] for j in range(8)]
        done = y[0] * lax.rsqrt(a[0, 0])
        for j in range(1, 8):
            done = jnp.where(sub == j, y[j] * lax.rsqrt(a[j, j]), done)
        out.append(jnp.where(lane < 8 * s + 8, done, 0.0))
        if s == 15:
            break
        q = [None] * 8
        for j in range(7, -1, -1):
            q[j] = z[j]
            for i in range(j + 1, 8):
                q[j] = q[j] - low[i, j] * q[i]
        for t in range(s + 1, 16):
            col = [over_lanes(tiles[t], 8 * s + c) for c in range(8)]
            acc = jnp.where(inside, 0.0, tiles[t])
            if t == s + 1:
                for j in range(8):
                    for i in range(j + 1, 8):
                        col[i] = col[i] - low[i, j] * col[j]
                for j in range(8):
                    acc = acc - col[j] * z[j]
                diag = [over_lanes(tiles[t], 8 * t + c) for c in range(8)]
                for j in range(8):
                    scaled = col[j] * inv[j]
                    for c in range(8):
                        diag[c] = diag[c] - col[j] * over_rows(scaled, c)
            else:
                for j in range(8):
                    acc = acc - col[j] * q[j]
            tiles[t] = acc
    return out


def assemble(g_ref, w):
    eye = jnp.where(
        lax.broadcasted_iota(jnp.int32, (NB, NB), 0) == lax.broadcasted_iota(jnp.int32, (NB, NB), 1), RIDGE, 0.0)
    for d in range(4):
        for b in range(NBLK):
            c = (b + d) % NBLK
            block = g_ref[d // 2, d % 2, b * NB:(b + 1) * NB, :]
            if d == 0:
                block = block + eye
            if b <= c:
                w[b * NB:(b + 1) * NB, c * NB:(c + 1) * NB] = block
            else:
                w[c * NB:(c + 1) * NB, b * NB:(b + 1) * NB] = block.T


def times_inverse(left, w, k):
    n = (k + 1) * NB
    return lax.dot_general(
        left[:, :n], w[k * NB:n, :n], (((1,), (1,)), ((), ())), precision=HI, preferred_element_type=F32)


def block(i):
    return slice(i * NB, (i + 1) * NB)


def dot_rows(a, b):
    return lax.dot_general(a, b, (((0,), (0,)), ((), ())), precision=HI, preferred_element_type=F32)


def split(x):
    high = x.astype(BF16)
    rest = x - high.astype(F32)
    mid = rest.astype(BF16)
    return high, mid, (rest - mid.astype(F32)).astype(BF16)


def terms(x):
    high, mid, low = split(x)
    return (high, mid, high, low, high, mid), (high, high, mid, high, low, mid)


def factor(w, lefts, rights, beside):
    w[pl.ds(RANK, NB), :] = jnp.zeros((NB, RANK), F32)
    lefts[:, pl.ds(RANK, NB)] = jnp.zeros((6 * NB, NB), BF16)

    def step(k, _):
        o = pl.multiple_of(k * NB, NB)
        at = pl.ds(o, NB)
        inv = jnp.concatenate(
            factor128([w[pl.ds(pl.multiple_of(o + 8 * t, 8), 8), at] for t in range(16)]), axis=0)
        left = jnp.concatenate(terms(inv)[0], axis=1)
        right = jnp.concatenate(terms(w[at, :])[1], axis=0)
        w[at, :] = jnp.dot(left, right, preferred_element_type=F32)
        w[at, at] = inv
        left, right = terms(w[at, :])
        for i in range(6):
            lefts[block(i), pl.ds(0, RANK)] = left[i]
            rights[block(i), :] = right[i]

        def update(i, _):
            below = pl.ds(pl.multiple_of((k + 1 + 2 * i) * NB, NB), 2 * NB)
            w[below, at] = jnp.zeros((2 * NB, NB), F32)
            w[below, :] -= lax.dot_general(
                lefts[:, below], rights[...], (((0,), (0,)), ((), ())), preferred_element_type=F32)
            return 0

        lax.fori_loop(0, (NBLK - k) // 2, update, 0)
        for when, act in beside.items():
            pl.when(k == when)(act)
        return 0

    lax.fori_loop(0, NBLK, step, 0)


OWN = 7
COPIES = 3 + 1 + 6 + 6 + 5 + 3 + 6 + 6 + 8 + 1 + 3 + 7 + 7 + 3 + 15 + 15 + 7 + 3 + 3 + 7 + 2


def step_kernel(mom_any, grad_any, basis_any, low_out, nb_out, pp, prx, pc, pf, ga, r1, s1, r2, zin, zp, zr, zt, a4, gf, low,
                so, sr, s, w, ra1, sa, ra2, ring_up, ring_down, acc_up, acc_down, sb, rb2, sq1, sq2, nb, xf,
                lefts, rights, mom, grad, basis, in_sem, ssem, rsem):
    inputs = [pltpu.make_async_copy(src, dst, in_sem.at[i])
              for i, (src, dst) in enumerate(((mom_any, mom), (grad_any, grad), (basis_any, basis)))]
    for copy in inputs:
        copy.start()
    lk = Links()
    cp = Copies(ssem, rsem)
    barrier, partners = greet(lk, "ZX")
    n = pp.shape[0]
    part = n // NX
    core_dev = lk.at_core()[1]

    def project(h):
        at = pl.ds(pl.multiple_of(h * (n // 2), 16), n // 2)
        low[at, :] = (mom[at, :] + grad[at, :].astype(F32)).astype(BF16)
        pp[at, :] = jnp.dot(low[at, :], basis[...], preferred_element_type=F32)

    for copy in inputs:
        copy.wait()
    mine_half = lk.x // 2
    project(1 - mine_half)
    pl.semaphore_wait(barrier, partners)
    sent = []
    for i in range(2):
        t = (1 - mine_half) * 2 + i
        slot = lax.rem(t - lk.x + NX, NX) - 1
        sent.append(cp.start(pp.at[rows(t * part, part)], prx.at[slot], {"tp": t}, slot=slot))
    project(mine_half)
    t = mine_half * 2 + 1 - lax.rem(lk.x, 2)
    slot = lax.rem(t - lk.x + NX, NX) - 1
    sent.append(cp.start(pp.at[rows(t * part, part)], prx.at[slot], {"tp": t}, slot=slot))
    for copy in sent:
        copy.wait_recv()
    mine = pp[rows(lk.x * part, part), :] + prx[0] + prx[1] + prx[2]
    pf[rows(lk.x * part, part), :] = mine
    pc[rows(lk.core * part, part), pl.ds(0, RANK)] = mine
    own = pc.at[rows(lk.core * part, part), pl.ds(0, RANK)]
    copy = cp.start(own, own, core_dev)
    copy.wait_recv()
    pc[:, pl.ds(RANK, 3 * NB)] = pc[:, pl.ds(0, 3 * NB)]

    for b in range(NBLK):
        blocks = dot_rows(pc[:, pl.ds(b * NB, NB)],
                          pc[:, pl.ds(pl.multiple_of((b + 2 * lk.core) * NB, NB), 2 * NB)])
        ga[0, pl.ds(b * NB, NB), :] = blocks[:, :NB]
        ga[1, pl.ds(b * NB, NB), :] = blocks[:, NB:]

    big, small = RANK // 4, RANK // 16
    sent = []
    for d in range(1, 4):
        tx, dx = lk.at_x(d)
        ty, dy = lk.at_y(d)
        sent.append(cp.start(ga.at[0, rows(tx * big, big)], r1.at[0, d - 1], dx))
        sent.append(cp.start(ga.at[1, rows(ty * big, big)], r1.at[1, d - 1], dy))
    for copy in sent:
        copy.wait_recv()
    s1[0] = ga[0, rows(lk.x * big, big), :] + r1[0, 0] + r1[0, 1] + r1[0, 2]
    s1[1] = ga[1, rows(lk.y * big, big), :] + r1[1, 0] + r1[1, 1] + r1[1, 2]
    sent = []
    for d in range(1, 4):
        tx, dx = lk.at_x(d)
        ty, dy = lk.at_y(d)
        sent.append(cp.start(s1.at[0, rows(ty * small, small)], r2.at[0, d - 1], dy))
        sent.append(cp.start(s1.at[1, rows(tx * small, small)], r2.at[1, d - 1], dx))
    rest = []
    own = pf.at[rows(lk.x * part, part)]
    for d in range(1, NX):
        rest.append(cp.start(own, own, lk.at_x(d)[1]))
    for copy in sent:
        copy.wait_recv()
    zin[0] = s1[0, rows(lk.y * small, small), :] + r2[0, 0] + r2[0, 1] + r2[0, 2]
    zin[1] = s1[1, rows(lk.x * small, small), :] + r2[1, 0] + r2[1, 1] + r2[1, 2]
    even = lax.rem(lk.z, 2)
    pair = lk.at_z(NZ + 1 - 2 * even)[1]
    copy = cp.start(zin.at[1 - even], zp, pair)
    copy.wait_recv()
    zr[lk.z // 2] = zin[even] + zp[...]
    sent = [cp.start(zr.at[lk.z // 2], zr.at[lk.z // 2], lk.at_z(d)[1]) for d in (2, 4, 6)]
    for copy in sent:
        copy.wait_recv()
    zt[even] = zr[0] + zr[1] + zr[2] + zr[3]
    copy = cp.start(zt.at[even], zt.at[even], pair)
    copy.wait_recv()

    a4[0, rows(lk.y * small, small), :] = zt[0]
    a4[1, rows(lk.x * small, small), :] = zt[1]
    sent = []
    for d in range(1, 4):
        own0 = a4.at[0, rows(lk.y * small, small)]
        own1 = a4.at[1, rows(lk.x * small, small)]
        sent.append(cp.start(own0, own0, lk.at_y(d)[1]))
        sent.append(cp.start(own1, own1, lk.at_x(d)[1]))
    for copy in sent:
        copy.wait_recv()
    gf[lk.core, 0, rows(lk.x * big, big), :] = a4[0]
    gf[lk.core, 1, rows(lk.y * big, big), :] = a4[1]
    own0 = gf.at[lk.core, 0, rows(lk.x * big, big)]
    own1 = gf.at[lk.core, 1, rows(lk.y * big, big)]
    sent = []
    for d in range(1, 4):
        sent.append((cp.start(own0, own0, lk.at_x(d)[1]), 0, lax.rem(lk.x + 4 - d, 4)))
        sent.append((cp.start(own1, own1, lk.at_y(d)[1]), 1, lax.rem(lk.y + 4 - d, 4)))
    across = [cp.start(own0, own0, core_dev), cp.start(own1, own1, core_dev)]
    for copy in rest:
        copy.wait_recv()
    so[...] = cross_half(low, pf, 1 - lk.core)
    cross = cp.start(so, sr, core_dev)
    s[...] = cross_half(low, pf, lk.core)
    for copy, h, t in sent:
        copy.wait_recv()
        piece = gf.at[lk.core, h, rows(t * big, big)]
        across.append(cp.start(piece, piece, core_dev))
    cross.wait_recv()
    s[...] += sr[...]

    half = RANK // 2
    ya, za, piece = half // NY, half // OWN, half // NY // OWN
    owner = lk.z < OWN
    zc = jnp.minimum(lk.z, OWN - 1)

    def ring_rows(shift):
        return rows(half + jnp.minimum(lax.rem(lk.z + NZ + shift, NZ), OWN - 1) * za, za)

    up, down = lk.at_z(1)[1], lk.at_z(NZ - 1)[1]
    ups = [cp.make(s.at[ring_rows(4)] if i == 0 else acc_up.at[i - 1], ring_up.at[i], up) for i in range(4)]
    downs = [cp.make(s.at[ring_rows(-3)] if i == 0 else acc_down.at[i - 1], ring_down.at[i], down) for i in range(3)]
    first_a = []
    for d in range(1, NY):
        t, dev = lk.at_y(d)
        first_a.append(cp.make(s.at[rows(t * ya, ya)], ra1.at[d - 1], dev))
    second_a = []
    for d in range(1, NZ):
        t, dev = lk.at_z(d)
        src = sa.at[rows(jnp.minimum(t, OWN - 1) * piece, piece)]
        second_a.append(cp.make(src, ra2.at[d - 1], dev))
    ring_at = {shift: ring_rows(shift) for shift in (3, 2, 1, -2, -1)}
    own_ya = rows(lk.y * ya, ya)

    def ring_step(i):
        ups[i - 1].wait_recv()
        acc_up[i - 1] = s[ring_at[4 - i], :] + ring_up[i - 1]
        ups[i].start()
        if i < 3:
            downs[i - 1].wait_recv()
            acc_down[i - 1] = s[ring_at[i - 3], :] + ring_down[i - 1]
            downs[i].start()

    def turn_a():
        for copy in first_a:
            copy.wait_recv()
        sa[...] = s[own_ya, :] + ra1[0] + ra1[1] + ra1[2]
        for copy in second_a:
            copy.start()

    for copy in [ups[0], downs[0]] + first_a:
        copy.start()
    for copy in across:
        copy.wait_recv()
    assemble(gf, w)
    factor(w, lefts, rights, {0: lambda: ring_step(1), 2: lambda: ring_step(2), 3: turn_a, 4: lambda: ring_step(3)})
    ups[-1].wait_recv()
    downs[-1].wait_recv()
    sb[...] = s[rows(half + zc * za, za), :] + ring_up[3] + ring_down[2]
    second_b = []
    for d in range(1, NY):
        t, dev = lk.at_y(d)
        second_b.append(cp.start(sb.at[rows(t * piece, piece)], rb2.at[d - 1], dev))
    for copy in second_b:
        copy.wait_recv()
    left_b = sb[rows(lk.y * piece, piece), :] + rb2[0] + rb2[1] + rb2[2]
    for copy in second_a:
        copy.wait_recv()
    left_a = sa[rows(zc * piece, piece), :]
    for i in range(NZ - 1):
        left_a = left_a + ra2[i]

    left = jnp.concatenate([left_a, left_b], axis=0)
    right = [times_inverse(left, w, k) for k in range(NBLK)]
    me1 = lk.z * 2 + lk.core
    me2 = lk.x * NY + lk.y
    base = lk.core * RANK
    at_a = rows16(base + lk.y * ya + zc * piece, piece)
    at_b = rows16(base + half + zc * za + lk.y * piece, piece)
    for k in range(NBLK):
        rounded = right[k].astype(BF16)

        @pl.when(owner)
        def _():
            nb[at_a, block(k)] = rounded[:piece]
            nb[at_b, block(k)] = rounded[piece:]

        sq1[me1, k:k + 1, :] = jnp.where(owner, jnp.sum(right[k] * right[k], axis=0, keepdims=True), 0.0)
    sq1[me1, NBLK:, :] = jnp.zeros((1, NB), F32)
    own = nb.at[at_b]
    gather_b = [cp.start(own, own, lk.at_y(d)[1], when=owner) for d in range(1, NY)]
    own = nb.at[at_a]
    gather_a = [cp.start(own, own, lk.at_z(d)[1], when=owner) for d in range(1, NZ)]
    squares = [cp.start(sq1.at[me1], sq1.at[me1], lk.at_zc(d)[1]) for d in range(1, 2 * NZ)]

    def owned(shift):
        return lax.rem(lk.z + NZ + shift, NZ) < OWN

    def part_b(shift):
        return nb.at[rows16(base + half + jnp.minimum(lax.rem(lk.z + NZ + shift, NZ), OWN - 1) * za, za)]

    @pl.when(owner)
    def _():
        for copy in gather_b:
            copy.wait_recv()

    ups = [cp.start(part_b(0), part_b(0), up, when=owned(0))]
    downs = [cp.start(part_b(0), part_b(0), down, when=owned(0))]

    def gather_step(i):
        pl.when(owned(-i))(ups[-1].wait_recv)
        ups.append(cp.start(part_b(-i), part_b(-i), up, when=owned(-i)))
        if i < 3:
            pl.when(owned(i))(downs[-1].wait_recv)
            downs.append(cp.start(part_b(i), part_b(i), down, when=owned(i)))

    for d in range(1, NZ):
        pl.when(owned(-d))(gather_a[d - 1].wait_recv)
    own = nb.at[rows16(base + lk.y * ya, ya)]
    gather_a = [cp.start(own, own, lk.at_y(d)[1]) for d in range(1, NY)]
    for copy in squares:
        copy.wait_recv()
    total = sq1[0]
    for i in range(1, 2 * NZ):
        total = total + sq1[i]
    sq2[me2] = total
    squares = [cp.start(sq2.at[me2], sq2.at[me2], lk.at_xy(dx, dy)[1])
               for dx in range(NX) for dy in range(NY) if dx or dy]
    gather_step(1)
    for k in range(4):
        xf[:, block(k)] = times_inverse(pf[...], w, k)
    gather_step(2)
    for k in range(4, 6):
        xf[:, block(k)] = times_inverse(pf[...], w, k)
    gather_step(3)
    for k in range(6, NBLK):
        xf[:, block(k)] = times_inverse(pf[...], w, k)
    for copy in gather_a:
        copy.wait_recv()
    own = nb.at[rows16(base, half)]
    across = [cp.start(own, own, core_dev)]
    for copy in squares:
        copy.wait_recv()
    total = sq2[0]
    for i in range(1, NX * NY):
        total = total + sq2[i]
    rms = jnp.sqrt(total / COLS_D + EPS)
    for k in range(NBLK):
        ortho = xf[:, block(k)]
        low_out[:n, block(k)] = (ortho * rms[k:k + 1, :]).astype(BF16)
        low_out[n:, block(k)] = ortho.astype(BF16)
    pl.when(owned(-4))(ups[-1].wait_recv)
    pl.when(owned(3))(downs[-1].wait_recv)
    own = nb.at[rows16(base + half, half)]
    across.append(cp.start(own, own, core_dev))
    scale = 1.0 / rms

    def normalize(start, size):
        at = rows16(start, size)
        for k in range(NBLK):
            nb_out[at, block(k)] = (nb[at, block(k)].astype(F32) * scale[k:k + 1, :]).astype(BF16)

    normalize(base, RANK)
    for i, copy in enumerate(across):
        copy.wait_recv()
        normalize((1 - lk.core) * RANK + i * half, half)
    cp.finish()


def rows16(start, size):
    return pl.ds(pl.multiple_of(start, 16), size)


def dion(momentum, gradient, basis):
    n, columns = momentum.shape
    vm = pl.BlockSpec(memory_space=pltpu.VMEM)
    half, big, small = RANK // 2, RANK // 4, RANK // 16
    ya, za, piece = half // NY, half // OWN, half // NY // OWN

    def buffer(*shape, dtype=F32):
        return pltpu.VMEM(shape, dtype)

    return pl.pallas_call(
        step_kernel,
        out_shape=(jax.ShapeDtypeStruct((2 * n, RANK), BF16), jax.ShapeDtypeStruct((columns, RANK), BF16)),
        in_specs=[pl.BlockSpec(memory_space=pl.ANY)] * 3,
        out_specs=(vm, vm),
        scratch_shapes=[
            buffer(n, RANK), buffer(3, n // NX, RANK), buffer(2 * n // NX, RANK + 3 * NB), buffer(n, RANK),
            buffer(2, RANK, NB), buffer(2, 3, big, NB), buffer(2, big, NB), buffer(2, 3, small, NB),
            buffer(2, small, NB), buffer(small, NB), buffer(4, small, NB), buffer(2, small, NB),
            buffer(2, big, NB), buffer(2, 2, RANK, NB), buffer(n, columns, dtype=BF16),
            buffer(RANK, RANK), buffer(RANK, RANK), buffer(RANK, RANK), buffer(RANK + NB, RANK),
            buffer(NY - 1, ya, RANK), buffer(ya, RANK), buffer(NZ - 1, piece, RANK),
            buffer(4, za, RANK), buffer(3, za, RANK), buffer(3, za, RANK), buffer(2, za, RANK),
            buffer(za, RANK), buffer(NY - 1, piece, RANK),
            buffer(2 * NZ, 8, NB), buffer(NX * NY, 8, NB), buffer(columns, RANK, dtype=BF16),
            buffer(n, RANK),
            buffer(6 * NB, RANK + NB, dtype=BF16), buffer(6 * NB, RANK, dtype=BF16),
            buffer(n, columns), buffer(n, columns, dtype=BF16), buffer(columns, RANK, dtype=BF16),
            pltpu.SemaphoreType.DMA((3,)),
            pltpu.SemaphoreType.DMA((COPIES,)), pltpu.SemaphoreType.DMA((COPIES,)),
        ],
        compiler_params=pltpu.CompilerParams(
            collective_id=0, has_side_effects=True, vmem_limit_bytes=60 * 2**20),
    )(momentum, gradient, basis)


def close_kernel(low, basis, mom, grad, mom_out, update_out, basis_out):
    n = mom.shape[0]
    products = lax.dot_general(low[...], basis[...], (((1,), (1,)), ((), ())), preferred_element_type=F32)
    mom_out[...] = mom[...] + grad[...].astype(F32) - (1.0 - DECAY) * products[:n]
    update_out[...] = (math.sqrt(ROWS_FF / RANK) * products[n:]).astype(BF16)
    basis_out[...] = basis[...]


def close(low, basis, momentum, gradient):
    n, columns = momentum.shape
    width = 2 * NB
    across = pl.BlockSpec((n, width), lambda j: (0, j))
    along = pl.BlockSpec((width, RANK), lambda j: (j, 0))
    return pl.pallas_call(
        close_kernel,
        grid=(columns // width,),
        in_specs=[pl.BlockSpec((2 * n, RANK), lambda j: (0, 0)), along, across, across],
        out_specs=(across, across, along),
        out_shape=(jax.ShapeDtypeStruct((n, columns), F32), jax.ShapeDtypeStruct((n, columns), BF16),
                   jax.ShapeDtypeStruct((columns, RANK), BF16)),
        compiler_params=pltpu.CompilerParams(vmem_limit_bytes=32 * 2**20),
    )(low, basis, momentum, gradient)


def body(momentum, gradient, column_basis):
    low, new_basis = dion(momentum, gradient, column_basis)
    return close(low, new_basis, momentum, gradient)


def solution(mesh):
    placed = (P("fsdp", "tp"), P("fsdp", "tp"), P("tp", None))
    return jax.shard_map(
        body,
        mesh=mesh,
        in_specs=placed,
        out_specs=(P("fsdp", "tp"), P("fsdp", "tp"), P("tp", None)),
        check_vma=False,
    )
```

```python
import math

import jax
import jax.numpy as jnp
from jax import lax
from jax.experimental import pallas as pl
from jax.experimental.pallas import tpu as pltpu
from jax.sharding import PartitionSpec as P

ROWS_FF = 18432
COLS_D = 7168
RANK = 896

RIDGE = 0.001
DECAY = 0.8
EPS = 1e-06
HI = lax.Precision.HIGHEST
F32 = jnp.float32
BF16 = jnp.bfloat16
NB = 128
NBLK = RANK // NB
MESH = pl.DeviceIdType.MESH
NX, NY, NZ = 4, 4, 8


class Links:
    def __init__(self):
        f = lax.axis_index("fsdp")
        self.x = lax.axis_index("tp")
        self.core = lax.rem(f, 2)
        self.z = lax.rem(f // 2, NZ)
        self.y = f // (2 * NZ)

    def at_x(self, d):
        t = lax.rem(self.x + d, NX)
        return t, {"tp": t}

    def at_y(self, d):
        t = lax.rem(self.y + d, NY)
        return t, {"fsdp": (t * NZ + self.z) * 2 + self.core}

    def at_z(self, d):
        t = lax.rem(self.z + d, NZ)
        return t, {"fsdp": (self.y * NZ + t) * 2 + self.core}

    def at_zc(self, d):
        t = lax.rem(self.z * 2 + self.core + d, 2 * NZ)
        return t, {"fsdp": self.y * NZ * 2 + t}

    def at_xy(self, dx, dy):
        tx, ty = lax.rem(self.x + dx, NX), lax.rem(self.y + dy, NY)
        return tx * NY + ty, {"tp": tx, "fsdp": (ty * NZ + self.z) * 2 + self.core}

    def at_core(self):
        t = 1 - self.core
        return t, {"fsdp": (self.y * NZ + self.z) * 2 + t}


class Copies:
    def __init__(self, send_sems, recv_sems):
        self.send_sems, self.recv_sems = send_sems, recv_sems
        self.count = 0
        self.started = []

    def make(self, src, dst, device, when=None, slot=None):
        arrival = self.count if slot is None else slot
        copy = pltpu.make_async_remote_copy(
            src_ref=src, dst_ref=dst, send_sem=self.send_sems.at[self.count],
            recv_sem=self.recv_sems.at[arrival], device_id=device, device_id_type=MESH)
        self.count += 1
        self.started.append((copy, when))
        return copy

    def start(self, src, dst, device, when=None, slot=None):
        copy = self.make(src, dst, device, when, slot)
        if when is None:
            copy.start()
        else:
            pl.when(when)(copy.start)
        return copy

    def finish(self):
        for copy, when in self.started:
            if when is None:
                copy.wait_send()
            else:
                pl.when(when)(copy.wait_send)
        self.started = []


def greet(links, along):
    barrier = pltpu.get_barrier_semaphore()
    partners = []
    if "x" in along:
        partners += [links.at_x(d)[1] for d in range(1, NX)]
    if "y" in along:
        partners += [links.at_y(d)[1] for d in range(1, NY)]
    if "z" in along:
        partners += [links.at_z(d)[1] for d in range(1, NZ)]
    if "c" in along:
        partners += [links.at_core()[1]]
    if "Z" in along:
        partners += [links.at_zc(d)[1] for d in range(1, 2 * NZ)]
    if "X" in along:
        partners += [links.at_xy(dx, dy)[1] for dx in range(NX) for dy in range(NY) if dx or dy]
    for device in partners:
        pl.semaphore_signal(barrier, inc=1, device_id=device, device_id_type=MESH)
    return barrier, len(partners)


def rows(start, size):
    return pl.ds(pl.multiple_of(start, 8), size)


def cross_half(low, projected, half):
    lhs = low[:, pl.ds(pl.multiple_of(half * RANK, NB), RANK)]
    p = projected[...]
    high = p.astype(BF16)
    rest = (p - high.astype(F32)).astype(BF16)
    dims = (((0,), (0,)), ((), ()))
    return (lax.dot_general(lhs, high, dims, preferred_element_type=F32)
            + lax.dot_general(lhs, rest, dims, preferred_element_type=F32))


def factor128(tiles):
    lane = lax.broadcasted_iota(jnp.int32, (8, 128), 1)
    sub = lax.broadcasted_iota(jnp.int32, (8, 128), 0)
    tiles = list(tiles)
    out = []

    def over_lanes(x, c):
        return jnp.broadcast_to(x[:, c:c + 1], (8, 128))

    def over_rows(x, r):
        return jnp.broadcast_to(x[r:r + 1, :], (8, 128))

    diag = [over_lanes(tiles[0], c) for c in range(8)]
    for s in range(16):
        a = {(r, c): over_rows(diag[c], r) for c in range(8) for r in range(c, 8)}
        inside = (lane >= 8 * s) & (lane < 8 * s + 8)
        row = jnp.where(inside, jnp.where(lane - 8 * s == sub, 1.0, 0.0), tiles[s])
        y = [over_rows(row, r) for r in range(8)]
        inv, low = [None] * 8, {}
        for j in range(8):
            inv[j] = pl.reciprocal(a[j, j], approx=False)
            for i in range(j + 1, 8):
                low[i, j] = a[i, j] * inv[j]
            for i in range(j + 1, 8):
                for k in range(j + 1, i + 1):
                    a[i, k] = a[i, k] - low[i, j] * a[k, j]
            for i in range(j + 1, 8):
                y[i] = y[i] - low[i, j] * y[j]
        z = [y[j] * inv[j] for j in range(8)]
        done = y[0] * lax.rsqrt(a[0, 0])
        for j in range(1, 8):
            done = jnp.where(sub == j, y[j] * lax.rsqrt(a[j, j]), done)
        out.append(jnp.where(lane < 8 * s + 8, done, 0.0))
        if s == 15:
            break
        q = [None] * 8
        for j in range(7, -1, -1):
            q[j] = z[j]
            for i in range(j + 1, 8):
                q[j] = q[j] - low[i, j] * q[i]
        for t in range(s + 1, 16):
            col = [over_lanes(tiles[t], 8 * s + c) for c in range(8)]
            acc = jnp.where(inside, 0.0, tiles[t])
            if t == s + 1:
                for j in range(8):
                    for i in range(j + 1, 8):
                        col[i] = col[i] - low[i, j] * col[j]
                for j in range(8):
                    acc = acc - col[j] * z[j]
                diag = [over_lanes(tiles[t], 8 * t + c) for c in range(8)]
                for j in range(8):
                    scaled = col[j] * inv[j]
                    for c in range(8):
                        diag[c] = diag[c] - col[j] * over_rows(scaled, c)
            else:
                for j in range(8):
                    acc = acc - col[j] * q[j]
            tiles[t] = acc
    return out


def assemble(g_ref, w):
    eye = jnp.where(
        lax.broadcasted_iota(jnp.int32, (NB, NB), 0) == lax.broadcasted_iota(jnp.int32, (NB, NB), 1), RIDGE, 0.0)
    for d in range(4):
        for b in range(NBLK):
            c = (b + d) % NBLK
            block = g_ref[d // 2, d % 2, b * NB:(b + 1) * NB, :]
            if d == 0:
                block = block + eye
            if b <= c:
                w[b * NB:(b + 1) * NB, c * NB:(c + 1) * NB] = block
            else:
                w[c * NB:(c + 1) * NB, b * NB:(b + 1) * NB] = block.T


def two(x):
    high = x.astype(BF16)
    return high, (x - high.astype(F32)).astype(BF16)


def times_inverse(left, w, k):
    n = (k + 1) * NB
    high, low = two(left[:, :n])
    w_high, w_low = two(w[k * NB:n, :n])
    return lax.dot_general(
        jnp.concatenate([high, high, low], axis=1), jnp.concatenate([w_high, w_low, w_high], axis=1),
        (((1,), (1,)), ((), ())), preferred_element_type=F32)


def block(i):
    return slice(i * NB, (i + 1) * NB)


def dot_rows(a, b):
    return lax.dot_general(a, b, (((0,), (0,)), ((), ())), precision=HI, preferred_element_type=F32)


def split(x):
    high = x.astype(BF16)
    rest = x - high.astype(F32)
    mid = rest.astype(BF16)
    return high, mid, (rest - mid.astype(F32)).astype(BF16)


def terms(x):
    high, mid, low = split(x)
    return (high, mid, high, low, high, mid), (high, high, mid, high, low, mid)


def factor(w, lefts, rights, amid, beside):
    w[pl.ds(RANK, NB), :] = jnp.zeros((NB, RANK), F32)
    lefts[:, pl.ds(RANK, NB)] = jnp.zeros((6 * NB, NB), BF16)

    def step(k, _):
        o = pl.multiple_of(k * NB, NB)
        at = pl.ds(o, NB)
        inv = jnp.concatenate(
            factor128([w[pl.ds(pl.multiple_of(o + 8 * t, 8), 8), at] for t in range(16)]), axis=0)
        for when, act in amid.items():
            pl.when(k == when)(act)
        left = jnp.concatenate(terms(inv)[0], axis=1)
        right = jnp.concatenate(terms(w[at, :])[1], axis=0)
        w[at, :] = jnp.dot(left, right, preferred_element_type=F32)
        w[at, at] = inv
        left, right = terms(w[at, :])
        for i in range(6):
            lefts[block(i), pl.ds(0, RANK)] = left[i]
            rights[block(i), :] = right[i]

        def update(i, _):
            below = pl.ds(pl.multiple_of((k + 1 + 2 * i) * NB, NB), 2 * NB)
            w[below, at] = jnp.zeros((2 * NB, NB), F32)
            w[below, :] -= lax.dot_general(
                lefts[:, below], rights[...], (((0,), (0,)), ((), ())), preferred_element_type=F32)
            return 0

        lax.fori_loop(0, (NBLK - k) // 2, update, 0)
        for when, act in beside.items():
            pl.when(k == when)(act)
        return 0

    lax.fori_loop(0, NBLK, step, 0)


OWN = 7
COPIES = 3 + 1 + 6 + 6 + 5 + 3 + 6 + 6 + 8 + 1 + 3 + 7 + 7 + 3 + 15 + 15 + 7 + 3 + 3 + 7 + 2


def step_kernel(mom_any, grad_any, basis_any, low_out, nb_out, pp, prx, pc, pf, ga, r1, s1, r2, zin, zp, zr, zt, a4, gf, low,
                so, sr, s, w, ra1, sa, ra2, ring_up, ring_down, acc_up, acc_down, sb, rb2, sq1, sq2, nb, xf,
                lefts, rights, mom, grad, basis, in_sem, ssem, rsem):
    inputs = [pltpu.make_async_copy(src, dst, in_sem.at[i])
              for i, (src, dst) in enumerate(((mom_any, mom), (grad_any, grad), (basis_any, basis)))]
    for copy in inputs:
        copy.start()
    lk = Links()
    cp = Copies(ssem, rsem)
    barrier, partners = greet(lk, "ZX")
    n = pp.shape[0]
    part = n // NX
    core_dev = lk.at_core()[1]

    def project(h):
        at = pl.ds(pl.multiple_of(h * (n // 2), 16), n // 2)
        low[at, :] = (mom[at, :] + grad[at, :].astype(F32)).astype(BF16)
        pp[at, :] = jnp.dot(low[at, :], basis[...], preferred_element_type=F32)

    for copy in inputs:
        copy.wait()
    mine_half = lk.x // 2
    project(1 - mine_half)
    pl.semaphore_wait(barrier, partners)
    sent = []
    for i in range(2):
        t = (1 - mine_half) * 2 + i
        slot = lax.rem(t - lk.x + NX, NX) - 1
        sent.append(cp.start(pp.at[rows(t * part, part)], prx.at[slot], {"tp": t}, slot=slot))
    project(mine_half)
    t = mine_half * 2 + 1 - lax.rem(lk.x, 2)
    slot = lax.rem(t - lk.x + NX, NX) - 1
    sent.append(cp.start(pp.at[rows(t * part, part)], prx.at[slot], {"tp": t}, slot=slot))
    for copy in sent:
        copy.wait_recv()
    mine = pp[rows(lk.x * part, part), :] + prx[0] + prx[1] + prx[2]
    pf[rows(lk.x * part, part), :] = mine
    pc[rows(lk.core * part, part), pl.ds(0, RANK)] = mine
    own = pc.at[rows(lk.core * part, part), pl.ds(0, RANK)]
    copy = cp.start(own, own, core_dev)
    copy.wait_recv()
    pc[:, pl.ds(RANK, 3 * NB)] = pc[:, pl.ds(0, 3 * NB)]

    for b in range(NBLK):
        blocks = dot_rows(pc[:, pl.ds(b * NB, NB)],
                          pc[:, pl.ds(pl.multiple_of((b + 2 * lk.core) * NB, NB), 2 * NB)])
        ga[0, pl.ds(b * NB, NB), :] = blocks[:, :NB]
        ga[1, pl.ds(b * NB, NB), :] = blocks[:, NB:]

    big, small = RANK // 4, RANK // 16
    sent = []
    for d in range(1, 4):
        tx, dx = lk.at_x(d)
        ty, dy = lk.at_y(d)
        sent.append(cp.start(ga.at[0, rows(tx * big, big)], r1.at[0, d - 1], dx))
        sent.append(cp.start(ga.at[1, rows(ty * big, big)], r1.at[1, d - 1], dy))
    for copy in sent:
        copy.wait_recv()
    s1[0] = ga[0, rows(lk.x * big, big), :] + r1[0, 0] + r1[0, 1] + r1[0, 2]
    s1[1] = ga[1, rows(lk.y * big, big), :] + r1[1, 0] + r1[1, 1] + r1[1, 2]
    sent = []
    for d in range(1, 4):
        tx, dx = lk.at_x(d)
        ty, dy = lk.at_y(d)
        sent.append(cp.start(s1.at[0, rows(ty * small, small)], r2.at[0, d - 1], dy))
        sent.append(cp.start(s1.at[1, rows(tx * small, small)], r2.at[1, d - 1], dx))
    rest = []
    own = pf.at[rows(lk.x * part, part)]
    for d in range(1, NX):
        rest.append(cp.start(own, own, lk.at_x(d)[1]))
    for copy in sent:
        copy.wait_recv()
    zin[0] = s1[0, rows(lk.y * small, small), :] + r2[0, 0] + r2[0, 1] + r2[0, 2]
    zin[1] = s1[1, rows(lk.x * small, small), :] + r2[1, 0] + r2[1, 1] + r2[1, 2]
    even = lax.rem(lk.z, 2)
    pair = lk.at_z(NZ + 1 - 2 * even)[1]
    copy = cp.start(zin.at[1 - even], zp, pair)
    copy.wait_recv()
    zr[lk.z // 2] = zin[even] + zp[...]
    sent = [cp.start(zr.at[lk.z // 2], zr.at[lk.z // 2], lk.at_z(d)[1]) for d in (2, 4, 6)]
    for copy in sent:
        copy.wait_recv()
    zt[even] = zr[0] + zr[1] + zr[2] + zr[3]
    copy = cp.start(zt.at[even], zt.at[even], pair)
    copy.wait_recv()

    a4[0, rows(lk.y * small, small), :] = zt[0]
    a4[1, rows(lk.x * small, small), :] = zt[1]
    sent = []
    for d in range(1, 4):
        own0 = a4.at[0, rows(lk.y * small, small)]
        own1 = a4.at[1, rows(lk.x * small, small)]
        sent.append(cp.start(own0, own0, lk.at_y(d)[1]))
        sent.append(cp.start(own1, own1, lk.at_x(d)[1]))
    for copy in sent:
        copy.wait_recv()
    gf[lk.core, 0, rows(lk.x * big, big), :] = a4[0]
    gf[lk.core, 1, rows(lk.y * big, big), :] = a4[1]
    own0 = gf.at[lk.core, 0, rows(lk.x * big, big)]
    own1 = gf.at[lk.core, 1, rows(lk.y * big, big)]
    sent = []
    for d in range(1, 4):
        sent.append((cp.start(own0, own0, lk.at_x(d)[1]), 0, lax.rem(lk.x + 4 - d, 4)))
        sent.append((cp.start(own1, own1, lk.at_y(d)[1]), 1, lax.rem(lk.y + 4 - d, 4)))
    across = [cp.start(own0, own0, core_dev), cp.start(own1, own1, core_dev)]
    for copy in rest:
        copy.wait_recv()
    so[...] = cross_half(low, pf, 1 - lk.core)
    cross = cp.start(so, sr, core_dev)
    s[...] = cross_half(low, pf, lk.core)
    for copy, h, t in sent:
        copy.wait_recv()
        piece = gf.at[lk.core, h, rows(t * big, big)]
        across.append(cp.start(piece, piece, core_dev))
    cross.wait_recv()
    s[...] += sr[...]

    half = RANK // 2
    ya, za, piece = half // NY, half // OWN, half // NY // OWN
    owner = lk.z < OWN
    zc = jnp.minimum(lk.z, OWN - 1)

    def ring_rows(shift):
        return rows(half + jnp.minimum(lax.rem(lk.z + NZ + shift, NZ), OWN - 1) * za, za)

    up, down = lk.at_z(1)[1], lk.at_z(NZ - 1)[1]
    ups = [cp.make(s.at[ring_rows(4)] if i == 0 else acc_up.at[i - 1], ring_up.at[i], up) for i in range(4)]
    downs = [cp.make(s.at[ring_rows(-3)] if i == 0 else acc_down.at[i - 1], ring_down.at[i], down) for i in range(3)]
    first_a = []
    for d in range(1, NY):
        t, dev = lk.at_y(d)
        first_a.append(cp.make(s.at[rows(t * ya, ya)], ra1.at[d - 1], dev))
    second_a = []
    for d in range(1, NZ):
        t, dev = lk.at_z(d)
        src = sa.at[rows(jnp.minimum(t, OWN - 1) * piece, piece)]
        second_a.append(cp.make(src, ra2.at[d - 1], dev))
    ring_at = {shift: ring_rows(shift) for shift in (3, 2, 1, -2, -1)}
    own_ya = rows(lk.y * ya, ya)

    def ring_step(i):
        ups[i - 1].wait_recv()
        acc_up[i - 1] = s[ring_at[4 - i], :] + ring_up[i - 1]
        ups[i].start()
        if i < 3:
            downs[i - 1].wait_recv()
            acc_down[i - 1] = s[ring_at[i - 3], :] + ring_down[i - 1]
            downs[i].start()

    def turn_a():
        for copy in first_a:
            copy.wait_recv()
        sa[...] = s[own_ya, :] + ra1[0] + ra1[1] + ra1[2]
        for copy in second_a:
            copy.start()

    second_b = []
    for d in range(1, NY):
        t, dev = lk.at_y(d)
        second_b.append(cp.make(sb.at[rows(t * piece, piece)], rb2.at[d - 1], dev))
    own_za = rows(half + zc * za, za)

    def turn_b():
        ups[3].wait_recv()
        downs[2].wait_recv()
        sb[...] = s[own_za, :] + ring_up[3] + ring_down[2]
        for copy in second_b:
            copy.start()

    for copy in [ups[0], downs[0]] + first_a:
        copy.start()
    for copy in across:
        copy.wait_recv()
    assemble(gf, w)
    factor(w, lefts, rights, {3: turn_a},
           {0: lambda: ring_step(1), 1: lambda: ring_step(2), 2: lambda: ring_step(3), 5: turn_b})
    for copy in second_b:
        copy.wait_recv()
    left_b = sb[rows(lk.y * piece, piece), :] + rb2[0] + rb2[1] + rb2[2]
    for copy in second_a:
        copy.wait_recv()
    left_a = sa[rows(zc * piece, piece), :]
    for i in range(NZ - 1):
        left_a = left_a + ra2[i]

    left = jnp.concatenate([left_a, left_b], axis=0)
    right = [times_inverse(left, w, k) for k in range(NBLK)]
    me1 = lk.z * 2 + lk.core
    me2 = lk.x * NY + lk.y
    base = lk.core * RANK
    at_a = rows16(base + lk.y * ya + zc * piece, piece)
    at_b = rows16(base + half + zc * za + lk.y * piece, piece)
    for k in range(NBLK):
        rounded = right[k].astype(BF16)

        @pl.when(owner)
        def _():
            nb[at_a, block(k)] = rounded[:piece]
            nb[at_b, block(k)] = rounded[piece:]

        sq1[me1, k:k + 1, :] = jnp.where(owner, jnp.sum(right[k] * right[k], axis=0, keepdims=True), 0.0)
    sq1[me1, NBLK:, :] = jnp.zeros((1, NB), F32)
    own = nb.at[at_b]
    gather_b = [cp.start(own, own, lk.at_y(d)[1], when=owner) for d in range(1, NY)]
    own = nb.at[at_a]
    gather_a = [cp.start(own, own, lk.at_z(d)[1], when=owner) for d in range(1, NZ)]
    squares = [cp.start(sq1.at[me1], sq1.at[me1], lk.at_zc(d)[1]) for d in range(1, 2 * NZ)]

    def owned(shift):
        return lax.rem(lk.z + NZ + shift, NZ) < OWN

    def part_b(shift):
        return nb.at[rows16(base + half + jnp.minimum(lax.rem(lk.z + NZ + shift, NZ), OWN - 1) * za, za)]

    @pl.when(owner)
    def _():
        for copy in gather_b:
            copy.wait_recv()

    ups = [cp.start(part_b(0), part_b(0), up, when=owned(0))]
    downs = [cp.start(part_b(0), part_b(0), down, when=owned(0))]

    def gather_step(i):
        pl.when(owned(-i))(ups[-1].wait_recv)
        ups.append(cp.start(part_b(-i), part_b(-i), up, when=owned(-i)))
        if i < 3:
            pl.when(owned(i))(downs[-1].wait_recv)
            downs.append(cp.start(part_b(i), part_b(i), down, when=owned(i)))

    def ortho(first, last):
        for k in range(first, last):
            xf[:, block(k)] = times_inverse(pf[...], w, k)

    ortho(0, 4)
    gather_step(1)
    for d in range(1, NZ):
        pl.when(owned(-d))(gather_a[d - 1].wait_recv)
    own = nb.at[rows16(base + lk.y * ya, ya)]
    gather_a = [cp.start(own, own, lk.at_y(d)[1]) for d in range(1, NY)]
    for copy in squares:
        copy.wait_recv()
    total = sq1[0]
    for i in range(1, 2 * NZ):
        total = total + sq1[i]
    sq2[me2] = total
    squares = [cp.start(sq2.at[me2], sq2.at[me2], lk.at_xy(dx, dy)[1])
               for dx in range(NX) for dy in range(NY) if dx or dy]
    ortho(4, 6)
    gather_step(2)
    ortho(6, NBLK)
    gather_step(3)
    for copy in squares:
        copy.wait_recv()
    total = sq2[0]
    for i in range(1, NX * NY):
        total = total + sq2[i]
    rms = jnp.sqrt(total / COLS_D + EPS)
    for k in range(NBLK):
        low_out[:n, block(k)] = (xf[:, block(k)] * rms[k:k + 1, :]).astype(BF16)
        low_out[n:, block(k)] = xf[:, block(k)].astype(BF16)
    for copy in gather_a:
        copy.wait_recv()
    own = nb.at[rows16(base, half)]
    across = [cp.start(own, own, core_dev)]
    scale = 1.0 / rms

    def normalize(start, size):
        at = rows16(start, size)
        for k in range(NBLK):
            nb_out[at, block(k)] = (nb[at, block(k)].astype(F32) * scale[k:k + 1, :]).astype(BF16)

    normalize(base, half)
    pl.when(owned(-4))(ups[-1].wait_recv)
    pl.when(owned(3))(downs[-1].wait_recv)
    own = nb.at[rows16(base + half, half)]
    across.append(cp.start(own, own, core_dev))
    normalize(base + half, half)
    for i, copy in enumerate(across):
        copy.wait_recv()
        normalize((1 - lk.core) * RANK + i * half, half)
    cp.finish()


def rows16(start, size):
    return pl.ds(pl.multiple_of(start, 16), size)


def dion(momentum, gradient, basis):
    n, columns = momentum.shape
    vm = pl.BlockSpec(memory_space=pltpu.VMEM)
    half, big, small = RANK // 2, RANK // 4, RANK // 16
    ya, za, piece = half // NY, half // OWN, half // NY // OWN

    def buffer(*shape, dtype=F32):
        return pltpu.VMEM(shape, dtype)

    return pl.pallas_call(
        step_kernel,
        out_shape=(jax.ShapeDtypeStruct((2 * n, RANK), BF16), jax.ShapeDtypeStruct((columns, RANK), BF16)),
        in_specs=[pl.BlockSpec(memory_space=pl.ANY)] * 3,
        out_specs=(vm, vm),
        scratch_shapes=[
            buffer(n, RANK), buffer(3, n // NX, RANK), buffer(2 * n // NX, RANK + 3 * NB), buffer(n, RANK),
            buffer(2, RANK, NB), buffer(2, 3, big, NB), buffer(2, big, NB), buffer(2, 3, small, NB),
            buffer(2, small, NB), buffer(small, NB), buffer(4, small, NB), buffer(2, small, NB),
            buffer(2, big, NB), buffer(2, 2, RANK, NB), buffer(n, columns, dtype=BF16),
            buffer(RANK, RANK), buffer(RANK, RANK), buffer(RANK, RANK), buffer(RANK + NB, RANK),
            buffer(NY - 1, ya, RANK), buffer(ya, RANK), buffer(NZ - 1, piece, RANK),
            buffer(4, za, RANK), buffer(3, za, RANK), buffer(3, za, RANK), buffer(2, za, RANK),
            buffer(za, RANK), buffer(NY - 1, piece, RANK),
            buffer(2 * NZ, 8, NB), buffer(NX * NY, 8, NB), buffer(columns, RANK, dtype=BF16),
            buffer(n, RANK),
            buffer(6 * NB, RANK + NB, dtype=BF16), buffer(6 * NB, RANK, dtype=BF16),
            buffer(n, columns), buffer(n, columns, dtype=BF16), buffer(columns, RANK, dtype=BF16),
            pltpu.SemaphoreType.DMA((3,)),
            pltpu.SemaphoreType.DMA((COPIES,)), pltpu.SemaphoreType.DMA((COPIES,)),
        ],
        compiler_params=pltpu.CompilerParams(
            collective_id=0, has_side_effects=True, vmem_limit_bytes=60 * 2**20),
    )(momentum, gradient, basis)


def close_kernel(low, basis, mom, grad, mom_out, update_out, basis_out):
    n = mom.shape[0]
    products = lax.dot_general(low[...], basis[...], (((1,), (1,)), ((), ())), preferred_element_type=F32)
    mom_out[...] = mom[...] + grad[...].astype(F32) - (1.0 - DECAY) * products[:n]
    update_out[...] = (math.sqrt(ROWS_FF / RANK) * products[n:]).astype(BF16)
    basis_out[...] = basis[...]


def close(low, basis, momentum, gradient):
    n, columns = momentum.shape
    width = 2 * NB
    across = pl.BlockSpec((n, width), lambda j: (0, j))
    along = pl.BlockSpec((width, RANK), lambda j: (j, 0))
    return pl.pallas_call(
        close_kernel,
        grid=(columns // width,),
        in_specs=[pl.BlockSpec((2 * n, RANK), lambda j: (0, 0)), along, across, across],
        out_specs=(across, across, along),
        out_shape=(jax.ShapeDtypeStruct((n, columns), F32), jax.ShapeDtypeStruct((n, columns), BF16),
                   jax.ShapeDtypeStruct((columns, RANK), BF16)),
        compiler_params=pltpu.CompilerParams(vmem_limit_bytes=60 * 2**20),
    )(low, basis, momentum, gradient)


def body(momentum, gradient, column_basis):
    low, new_basis = dion(momentum, gradient, column_basis)
    return close(low, new_basis, momentum, gradient)


def solution(mesh):
    placed = (P("fsdp", "tp"), P("fsdp", "tp"), P("tp", None))
    return jax.shard_map(
        body,
        mesh=mesh,
        in_specs=placed,
        out_specs=(P("fsdp", "tp"), P("fsdp", "tp"), P("tp", None)),
        check_vma=False,
    )
```

```python
import math

import jax
import jax.numpy as jnp
from jax import lax
from jax.experimental import pallas as pl
from jax.experimental.pallas import tpu as pltpu
from jax.sharding import PartitionSpec as P

ROWS_FF = 18432
COLS_D = 7168
RANK = 896

RIDGE = 0.001
DECAY = 0.8
EPS = 1e-06
HI = lax.Precision.HIGHEST
F32 = jnp.float32
BF16 = jnp.bfloat16
NB = 128
NBLK = RANK // NB
MESH = pl.DeviceIdType.MESH
NX, NY, NZ = 4, 4, 8


class Links:
    def __init__(self):
        f = lax.axis_index("fsdp")
        self.x = lax.axis_index("tp")
        self.core = lax.rem(f, 2)
        self.z = lax.rem(f // 2, NZ)
        self.y = f // (2 * NZ)

    def at_x(self, d):
        t = lax.rem(self.x + d, NX)
        return t, {"tp": t}

    def at_y(self, d):
        t = lax.rem(self.y + d, NY)
        return t, {"fsdp": (t * NZ + self.z) * 2 + self.core}

    def at_z(self, d):
        t = lax.rem(self.z + d, NZ)
        return t, {"fsdp": (self.y * NZ + t) * 2 + self.core}

    def at_zc(self, d):
        t = lax.rem(self.z * 2 + self.core + d, 2 * NZ)
        return t, {"fsdp": self.y * NZ * 2 + t}

    def at_xy(self, dx, dy):
        tx, ty = lax.rem(self.x + dx, NX), lax.rem(self.y + dy, NY)
        return tx * NY + ty, {"tp": tx, "fsdp": (ty * NZ + self.z) * 2 + self.core}

    def at_core(self):
        t = 1 - self.core
        return t, {"fsdp": (self.y * NZ + self.z) * 2 + t}


class Copies:
    def __init__(self, send_sems, recv_sems):
        self.send_sems, self.recv_sems = send_sems, recv_sems
        self.count = 0
        self.started = []

    def make(self, src, dst, device, when=None, slot=None):
        arrival = self.count if slot is None else slot
        copy = pltpu.make_async_remote_copy(
            src_ref=src, dst_ref=dst, send_sem=self.send_sems.at[self.count],
            recv_sem=self.recv_sems.at[arrival], device_id=device, device_id_type=MESH)
        self.count += 1
        self.started.append((copy, when))
        return copy

    def start(self, src, dst, device, when=None, slot=None):
        copy = self.make(src, dst, device, when, slot)
        if when is None:
            copy.start()
        else:
            pl.when(when)(copy.start)
        return copy

    def finish(self):
        for copy, when in self.started:
            if when is None:
                copy.wait_send()
            else:
                pl.when(when)(copy.wait_send)
        self.started = []


def greet(links, along):
    barrier = pltpu.get_barrier_semaphore()
    partners = []
    if "x" in along:
        partners += [links.at_x(d)[1] for d in range(1, NX)]
    if "y" in along:
        partners += [links.at_y(d)[1] for d in range(1, NY)]
    if "z" in along:
        partners += [links.at_z(d)[1] for d in range(1, NZ)]
    if "c" in along:
        partners += [links.at_core()[1]]
    if "Z" in along:
        partners += [links.at_zc(d)[1] for d in range(1, 2 * NZ)]
    if "X" in along:
        partners += [links.at_xy(dx, dy)[1] for dx in range(NX) for dy in range(NY) if dx or dy]
    for device in partners:
        pl.semaphore_signal(barrier, inc=1, device_id=device, device_id_type=MESH)
    return barrier, len(partners)


def rows(start, size):
    return pl.ds(pl.multiple_of(start, 8), size)


def cross_half(low, projected, half):
    lhs = low[:, pl.ds(pl.multiple_of(half * RANK, NB), RANK)]
    p = projected[...]
    high = p.astype(BF16)
    rest = (p - high.astype(F32)).astype(BF16)
    dims = (((0,), (0,)), ((), ()))
    return (lax.dot_general(lhs, high, dims, preferred_element_type=F32)
            + lax.dot_general(lhs, rest, dims, preferred_element_type=F32))


def factor128(tiles):
    lane = lax.broadcasted_iota(jnp.int32, (8, 128), 1)
    sub = lax.broadcasted_iota(jnp.int32, (8, 128), 0)
    tiles = list(tiles)
    out = []

    def over_lanes(x, c):
        return jnp.broadcast_to(x[:, c:c + 1], (8, 128))

    def over_rows(x, r):
        return jnp.broadcast_to(x[r:r + 1, :], (8, 128))

    diag = [over_lanes(tiles[0], c) for c in range(8)]
    for s in range(16):
        a = {(r, c): over_rows(diag[c], r) for c in range(8) for r in range(c, 8)}
        inside = (lane >= 8 * s) & (lane < 8 * s + 8)
        row = jnp.where(inside, jnp.where(lane - 8 * s == sub, 1.0, 0.0), tiles[s])
        y = [over_rows(row, r) for r in range(8)]
        inv, low = [None] * 8, {}
        for j in range(8):
            inv[j] = pl.reciprocal(a[j, j], approx=False)
            for i in range(j + 1, 8):
                low[i, j] = a[i, j] * inv[j]
            for i in range(j + 1, 8):
                for k in range(j + 1, i + 1):
                    a[i, k] = a[i, k] - low[i, j] * a[k, j]
            for i in range(j + 1, 8):
                y[i] = y[i] - low[i, j] * y[j]
        z = [y[j] * inv[j] for j in range(8)]
        done = y[0] * lax.rsqrt(a[0, 0])
        for j in range(1, 8):
            done = jnp.where(sub == j, y[j] * lax.rsqrt(a[j, j]), done)
        out.append(jnp.where(lane < 8 * s + 8, done, 0.0))
        if s == 15:
            break
        q = [None] * 8
        for j in range(7, -1, -1):
            q[j] = z[j]
            for i in range(j + 1, 8):
                q[j] = q[j] - low[i, j] * q[i]
        for t in range(s + 1, 16):
            col = [over_lanes(tiles[t], 8 * s + c) for c in range(8)]
            acc = jnp.where(inside, 0.0, tiles[t])
            if t == s + 1:
                for j in range(8):
                    for i in range(j + 1, 8):
                        col[i] = col[i] - low[i, j] * col[j]
                for j in range(8):
                    acc = acc - col[j] * z[j]
                diag = [over_lanes(tiles[t], 8 * t + c) for c in range(8)]
                for j in range(8):
                    scaled = col[j] * inv[j]
                    for c in range(8):
                        diag[c] = diag[c] - col[j] * over_rows(scaled, c)
            else:
                for j in range(8):
                    acc = acc - col[j] * q[j]
            tiles[t] = acc
    return out


def assemble(g_ref, w):
    eye = jnp.where(
        lax.broadcasted_iota(jnp.int32, (NB, NB), 0) == lax.broadcasted_iota(jnp.int32, (NB, NB), 1), RIDGE, 0.0)
    for d in range(4):
        for b in range(NBLK):
            c = (b + d) % NBLK
            block = g_ref[d // 2, d % 2, b * NB:(b + 1) * NB, :]
            if d == 0:
                block = block + eye
            if b <= c:
                w[b * NB:(b + 1) * NB, c * NB:(c + 1) * NB] = block
            else:
                w[c * NB:(c + 1) * NB, b * NB:(b + 1) * NB] = block.T


def two(x):
    high = x.astype(BF16)
    return high, (x - high.astype(F32)).astype(BF16)


def times_inverse(left, w, k):
    n = (k + 1) * NB
    high, low = two(left[:, :n])
    w_high, w_low = two(w[k * NB:n, :n])
    return lax.dot_general(
        jnp.concatenate([high, high, low], axis=1), jnp.concatenate([w_high, w_low, w_high], axis=1),
        (((1,), (1,)), ((), ())), preferred_element_type=F32)


def block(i):
    return slice(i * NB, (i + 1) * NB)


def dot_rows(a, b):
    return lax.dot_general(a, b, (((0,), (0,)), ((), ())), precision=HI, preferred_element_type=F32)


def split(x):
    high = x.astype(BF16)
    rest = x - high.astype(F32)
    mid = rest.astype(BF16)
    return high, mid, (rest - mid.astype(F32)).astype(BF16)


def terms(x):
    high, mid, low = split(x)
    return (high, mid, high, low, high, mid), (high, high, mid, high, low, mid)


def factor(w, lefts, rights, amid, beside):
    w[pl.ds(RANK, NB), :] = jnp.zeros((NB, RANK), F32)
    lefts[:, pl.ds(RANK, NB)] = jnp.zeros((6 * NB, NB), BF16)

    def step(k, _):
        o = pl.multiple_of(k * NB, NB)
        at = pl.ds(o, NB)
        inv = jnp.concatenate(
            factor128([w[pl.ds(pl.multiple_of(o + 8 * t, 8), 8), at] for t in range(16)]), axis=0)
        for when, act in amid.items():
            pl.when(k == when)(act)
        left = jnp.concatenate(terms(inv)[0], axis=1)
        right = jnp.concatenate(terms(w[at, :])[1], axis=0)
        w[at, :] = jnp.dot(left, right, preferred_element_type=F32)
        w[at, at] = inv
        left, right = terms(w[at, :])
        for i in range(6):
            lefts[block(i), pl.ds(0, RANK)] = left[i]
            rights[block(i), :] = right[i]

        def update(i, _):
            below = pl.ds(pl.multiple_of((k + 1 + 2 * i) * NB, NB), 2 * NB)
            w[below, at] = jnp.zeros((2 * NB, NB), F32)
            w[below, :] -= lax.dot_general(
                lefts[:, below], rights[...], (((0,), (0,)), ((), ())), preferred_element_type=F32)
            return 0

        lax.fori_loop(0, (NBLK - k) // 2, update, 0)
        for when, act in beside.items():
            pl.when(k == when)(act)
        return 0

    lax.fori_loop(0, NBLK, step, 0)


OWN = 7
COPIES = 3 + 1 + 6 + 6 + 5 + 3 + 6 + 6 + 8 + 1 + 3 + 7 + 7 + 3 + 15 + 15 + 7 + 3 + 3 + 7 + 2 + 7


def step_kernel(mom_any, grad_any, basis_any, low_any, nb_any, pp, prx, pc, pf, ga, r1, s1, r2, zin, zp, zr, zt, a4, gf, low,
                so, sr, s, w, ra1, sa, ra2, ring_up, ring_down, acc_up, acc_down, sb, rb2, sq1, sq2, nb, xf,
                lefts, rights, mom, grad, basis, low_out, nb_out, in_sem, out_sem, ssem, rsem):
    inputs = [pltpu.make_async_copy(src, dst, in_sem.at[i])
              for i, (src, dst) in enumerate(((mom_any, mom), (grad_any, grad), (basis_any, basis)))]
    for copy in inputs:
        copy.start()
    lk = Links()
    cp = Copies(ssem, rsem)
    barrier, partners = greet(lk, "ZX")
    n = pp.shape[0]
    part = n // NX
    core_dev = lk.at_core()[1]

    def project(h):
        at = pl.ds(pl.multiple_of(h * (n // 2), 16), n // 2)
        low[at, :] = (mom[at, :] + grad[at, :].astype(F32)).astype(BF16)
        pp[at, :] = jnp.dot(low[at, :], basis[...], preferred_element_type=F32)

    for copy in inputs:
        copy.wait()
    mine_half = lk.x // 2
    project(1 - mine_half)
    pl.semaphore_wait(barrier, partners)
    sent = []
    for i in range(2):
        t = (1 - mine_half) * 2 + i
        slot = lax.rem(t - lk.x + NX, NX) - 1
        sent.append(cp.start(pp.at[rows(t * part, part)], prx.at[slot], {"tp": t}, slot=slot))
    project(mine_half)
    t = mine_half * 2 + 1 - lax.rem(lk.x, 2)
    slot = lax.rem(t - lk.x + NX, NX) - 1
    sent.append(cp.start(pp.at[rows(t * part, part)], prx.at[slot], {"tp": t}, slot=slot))
    for copy in sent:
        copy.wait_recv()
    mine = pp[rows(lk.x * part, part), :] + prx[0] + prx[1] + prx[2]
    pf[rows(lk.x * part, part), :] = mine
    pc[rows(lk.core * part, part), pl.ds(0, RANK)] = mine
    own = pc.at[rows(lk.core * part, part), pl.ds(0, RANK)]
    copy = cp.start(own, own, core_dev)
    copy.wait_recv()
    pc[:, pl.ds(RANK, 3 * NB)] = pc[:, pl.ds(0, 3 * NB)]

    for b in range(NBLK):
        blocks = dot_rows(pc[:, pl.ds(b * NB, NB)],
                          pc[:, pl.ds(pl.multiple_of((b + 2 * lk.core) * NB, NB), 2 * NB)])
        ga[0, pl.ds(b * NB, NB), :] = blocks[:, :NB]
        ga[1, pl.ds(b * NB, NB), :] = blocks[:, NB:]

    big, small = RANK // 4, RANK // 16
    sent = []
    for d in range(1, 4):
        tx, dx = lk.at_x(d)
        ty, dy = lk.at_y(d)
        sent.append(cp.start(ga.at[0, rows(tx * big, big)], r1.at[0, d - 1], dx))
        sent.append(cp.start(ga.at[1, rows(ty * big, big)], r1.at[1, d - 1], dy))
    for copy in sent:
        copy.wait_recv()
    s1[0] = ga[0, rows(lk.x * big, big), :] + r1[0, 0] + r1[0, 1] + r1[0, 2]
    s1[1] = ga[1, rows(lk.y * big, big), :] + r1[1, 0] + r1[1, 1] + r1[1, 2]
    sent = []
    for d in range(1, 4):
        tx, dx = lk.at_x(d)
        ty, dy = lk.at_y(d)
        sent.append(cp.start(s1.at[0, rows(ty * small, small)], r2.at[0, d - 1], dy))
        sent.append(cp.start(s1.at[1, rows(tx * small, small)], r2.at[1, d - 1], dx))
    rest = []
    own = pf.at[rows(lk.x * part, part)]
    for d in range(1, NX):
        rest.append(cp.start(own, own, lk.at_x(d)[1]))
    for copy in sent:
        copy.wait_recv()
    zin[0] = s1[0, rows(lk.y * small, small), :] + r2[0, 0] + r2[0, 1] + r2[0, 2]
    zin[1] = s1[1, rows(lk.x * small, small), :] + r2[1, 0] + r2[1, 1] + r2[1, 2]
    even = lax.rem(lk.z, 2)
    pair = lk.at_z(NZ + 1 - 2 * even)[1]
    copy = cp.start(zin.at[1 - even], zp, pair)
    copy.wait_recv()
    zr[lk.z // 2] = zin[even] + zp[...]
    sent = [cp.start(zr.at[lk.z // 2], zr.at[lk.z // 2], lk.at_z(d)[1]) for d in (2, 4, 6)]
    for copy in sent:
        copy.wait_recv()
    zt[even] = zr[0] + zr[1] + zr[2] + zr[3]
    copy = cp.start(zt.at[even], zt.at[even], pair)
    copy.wait_recv()

    a4[0, rows(lk.y * small, small), :] = zt[0]
    a4[1, rows(lk.x * small, small), :] = zt[1]
    sent = []
    for d in range(1, 4):
        own0 = a4.at[0, rows(lk.y * small, small)]
        own1 = a4.at[1, rows(lk.x * small, small)]
        sent.append(cp.start(own0, own0, lk.at_y(d)[1]))
        sent.append(cp.start(own1, own1, lk.at_x(d)[1]))
    for copy in sent:
        copy.wait_recv()
    gf[lk.core, 0, rows(lk.x * big, big), :] = a4[0]
    gf[lk.core, 1, rows(lk.y * big, big), :] = a4[1]
    own0 = gf.at[lk.core, 0, rows(lk.x * big, big)]
    own1 = gf.at[lk.core, 1, rows(lk.y * big, big)]
    sent = []
    for d in range(1, 4):
        sent.append((cp.start(own0, own0, lk.at_x(d)[1]), 0, lax.rem(lk.x + 4 - d, 4)))
        sent.append((cp.start(own1, own1, lk.at_y(d)[1]), 1, lax.rem(lk.y + 4 - d, 4)))
    across = [cp.start(own0, own0, core_dev), cp.start(own1, own1, core_dev)]
    for copy in rest:
        copy.wait_recv()
    so[...] = cross_half(low, pf, 1 - lk.core)
    cross = cp.start(so, sr, core_dev)
    s[...] = cross_half(low, pf, lk.core)
    for copy, h, t in sent:
        copy.wait_recv()
        piece = gf.at[lk.core, h, rows(t * big, big)]
        across.append(cp.start(piece, piece, core_dev))
    cross.wait_recv()
    s[...] += sr[...]

    half = RANK // 2
    ya, za, piece = half // NY, half // OWN, half // NY // OWN
    owner = lk.z < OWN
    zc = jnp.minimum(lk.z, OWN - 1)

    def ring_rows(shift):
        return rows(half + jnp.minimum(lax.rem(lk.z + NZ + shift, NZ), OWN - 1) * za, za)

    up, down = lk.at_z(1)[1], lk.at_z(NZ - 1)[1]
    ups = [cp.make(s.at[ring_rows(4)] if i == 0 else acc_up.at[i - 1], ring_up.at[i], up) for i in range(4)]
    downs = [cp.make(s.at[ring_rows(-3)] if i == 0 else acc_down.at[i - 1], ring_down.at[i], down) for i in range(3)]
    first_a = []
    for d in range(1, NY):
        t, dev = lk.at_y(d)
        first_a.append(cp.make(s.at[rows(t * ya, ya)], ra1.at[d - 1], dev))
    second_a = []
    for d in range(1, NZ):
        t, dev = lk.at_z(d)
        src = sa.at[rows(jnp.minimum(t, OWN - 1) * piece, piece)]
        second_a.append(cp.make(src, ra2.at[d - 1], dev))
    ring_at = {shift: ring_rows(shift) for shift in (3, 2, 1, -2, -1)}
    own_ya = rows(lk.y * ya, ya)

    def ring_step(i):
        ups[i - 1].wait_recv()
        acc_up[i - 1] = s[ring_at[4 - i], :] + ring_up[i - 1]
        ups[i].start()
        if i < 3:
            downs[i - 1].wait_recv()
            acc_down[i - 1] = s[ring_at[i - 3], :] + ring_down[i - 1]
            downs[i].start()

    def turn_a():
        for copy in first_a:
            copy.wait_recv()
        sa[...] = s[own_ya, :] + ra1[0] + ra1[1] + ra1[2]
        for copy in second_a:
            copy.start()

    second_b = []
    for d in range(1, NY):
        t, dev = lk.at_y(d)
        second_b.append(cp.make(sb.at[rows(t * piece, piece)], rb2.at[d - 1], dev))
    own_za = rows(half + zc * za, za)

    def turn_b():
        ups[3].wait_recv()
        downs[2].wait_recv()
        sb[...] = s[own_za, :] + ring_up[3] + ring_down[2]
        for copy in second_b:
            copy.start()

    for copy in [ups[0], downs[0]] + first_a:
        copy.start()
    for copy in across:
        copy.wait_recv()
    assemble(gf, w)
    factor(w, lefts, rights, {3: turn_a},
           {0: lambda: ring_step(1), 1: lambda: ring_step(2), 2: lambda: ring_step(3), 5: turn_b})
    for copy in second_b:
        copy.wait_recv()
    left_b = sb[rows(lk.y * piece, piece), :] + rb2[0] + rb2[1] + rb2[2]
    for copy in second_a:
        copy.wait_recv()
    left_a = sa[rows(zc * piece, piece), :]
    for i in range(NZ - 1):
        left_a = left_a + ra2[i]

    left = jnp.concatenate([left_a, left_b], axis=0)
    right = [times_inverse(left, w, k) for k in range(NBLK)]
    me1 = lk.z * 2 + lk.core
    me2 = lk.x * NY + lk.y
    base = lk.core * RANK
    at_a = rows16(base + lk.y * ya + zc * piece, piece)
    at_b = rows16(base + half + zc * za + lk.y * piece, piece)
    for k in range(NBLK):
        rounded = right[k].astype(BF16)

        @pl.when(owner)
        def _():
            nb[at_a, block(k)] = rounded[:piece]
            nb[at_b, block(k)] = rounded[piece:]

        sq1[me1, k:k + 1, :] = jnp.where(owner, jnp.sum(right[k] * right[k], axis=0, keepdims=True), 0.0)
    sq1[me1, NBLK:, :] = jnp.zeros((1, NB), F32)
    own = nb.at[at_b]
    gather_b = [cp.start(own, own, lk.at_y(d)[1], when=owner) for d in range(1, NY)]
    own = nb.at[at_a]
    gather_a = [cp.start(own, own, lk.at_z(d)[1], when=owner) for d in range(1, NZ)]
    squares = [cp.start(sq1.at[me1], sq1.at[me1], lk.at_zc(d)[1]) for d in range(1, 2 * NZ)]

    def owned(shift):
        return lax.rem(lk.z + NZ + shift, NZ) < OWN

    def part_b(shift):
        return nb.at[rows16(base + half + jnp.minimum(lax.rem(lk.z + NZ + shift, NZ), OWN - 1) * za, za)]

    @pl.when(owner)
    def _():
        for copy in gather_b:
            copy.wait_recv()

    ups = [cp.start(part_b(0), part_b(0), up, when=owned(0))]
    downs = [cp.start(part_b(0), part_b(0), down, when=owned(0))]
    passed = []

    def pass_on(shift):
        piece_b = part_b(shift)
        passed.append((cp.start(piece_b, piece_b, core_dev, when=owned(shift)), owned(shift)))

    pass_on(0)

    def gather_step(i):
        pl.when(owned(-i))(ups[-1].wait_recv)
        ups.append(cp.start(part_b(-i), part_b(-i), up, when=owned(-i)))
        pass_on(-i)
        if i < 3:
            pl.when(owned(i))(downs[-1].wait_recv)
            downs.append(cp.start(part_b(i), part_b(i), down, when=owned(i)))
            pass_on(i)

    def ortho(first, last):
        for k in range(first, last):
            xf[:, block(k)] = times_inverse(pf[...], w, k)

    ortho(0, 4)
    gather_step(1)
    for d in range(1, NZ):
        pl.when(owned(-d))(gather_a[d - 1].wait_recv)
    own = nb.at[rows16(base + lk.y * ya, ya)]
    gather_a = [cp.start(own, own, lk.at_y(d)[1]) for d in range(1, NY)]
    for copy in squares:
        copy.wait_recv()
    total = sq1[0]
    for i in range(1, 2 * NZ):
        total = total + sq1[i]
    sq2[me2] = total
    squares = [cp.start(sq2.at[me2], sq2.at[me2], lk.at_xy(dx, dy)[1])
               for dx in range(NX) for dy in range(NY) if dx or dy]
    ortho(4, 6)
    gather_step(2)
    ortho(6, NBLK)
    gather_step(3)
    for copy in squares:
        copy.wait_recv()
    total = sq2[0]
    for i in range(1, NX * NY):
        total = total + sq2[i]
    rms = jnp.sqrt(total / COLS_D + EPS)
    for k in range(NBLK):
        low_out[:n, block(k)] = (xf[:, block(k)] * rms[k:k + 1, :]).astype(BF16)
        low_out[n:, block(k)] = xf[:, block(k)].astype(BF16)
    stores = [pltpu.make_async_copy(low_out, low_any, out_sem.at[4])]
    stores[0].start()
    for copy in gather_a:
        copy.wait_recv()
    own = nb.at[rows16(base, half)]
    across = [cp.start(own, own, core_dev)]
    scale = 1.0 / rms

    def normalize(start, size):
        at = rows16(start, size)
        for k in range(NBLK):
            nb_out[at, block(k)] = (nb[at, block(k)].astype(F32) * scale[k:k + 1, :]).astype(BF16)
        stores.append(pltpu.make_async_copy(nb_out.at[at], nb_any.at[at], out_sem.at[len(stores) - 1]))
        stores[-1].start()

    normalize(base, half)
    pl.when(owned(-4))(ups[-1].wait_recv)
    pl.when(owned(3))(downs[-1].wait_recv)
    pass_on(-4)
    pass_on(3)
    normalize(base + half, half)
    across[0].wait_recv()
    normalize((1 - lk.core) * RANK, half)
    for copy, arrives in passed:
        pl.when(arrives)(copy.wait_recv)
    normalize((1 - lk.core) * RANK + half, half)
    for copy in stores:
        copy.wait()
    cp.finish()


def rows16(start, size):
    return pl.ds(pl.multiple_of(start, 16), size)


def dion(momentum, gradient, basis):
    n, columns = momentum.shape
    half, big, small = RANK // 2, RANK // 4, RANK // 16
    ya, za, piece = half // NY, half // OWN, half // NY // OWN

    def buffer(*shape, dtype=F32):
        return pltpu.VMEM(shape, dtype)

    return pl.pallas_call(
        step_kernel,
        out_shape=(jax.ShapeDtypeStruct((2 * n, RANK), BF16), jax.ShapeDtypeStruct((columns, RANK), BF16)),
        in_specs=[pl.BlockSpec(memory_space=pl.ANY)] * 3,
        out_specs=(pl.BlockSpec(memory_space=pl.ANY),) * 2,
        scratch_shapes=[
            buffer(n, RANK), buffer(3, n // NX, RANK), buffer(2 * n // NX, RANK + 3 * NB), buffer(n, RANK),
            buffer(2, RANK, NB), buffer(2, 3, big, NB), buffer(2, big, NB), buffer(2, 3, small, NB),
            buffer(2, small, NB), buffer(small, NB), buffer(4, small, NB), buffer(2, small, NB),
            buffer(2, big, NB), buffer(2, 2, RANK, NB), buffer(n, columns, dtype=BF16),
            buffer(RANK, RANK), buffer(RANK, RANK), buffer(RANK, RANK), buffer(RANK + NB, RANK),
            buffer(NY - 1, ya, RANK), buffer(ya, RANK), buffer(NZ - 1, piece, RANK),
            buffer(4, za, RANK), buffer(3, za, RANK), buffer(3, za, RANK), buffer(2, za, RANK),
            buffer(za, RANK), buffer(NY - 1, piece, RANK),
            buffer(2 * NZ, 8, NB), buffer(NX * NY, 8, NB), buffer(columns, RANK, dtype=BF16),
            buffer(n, RANK),
            buffer(6 * NB, RANK + NB, dtype=BF16), buffer(6 * NB, RANK, dtype=BF16),
            buffer(n, columns), buffer(n, columns, dtype=BF16), buffer(columns, RANK, dtype=BF16),
            buffer(2 * n, RANK, dtype=BF16), buffer(columns, RANK, dtype=BF16),
            pltpu.SemaphoreType.DMA((3,)), pltpu.SemaphoreType.DMA((5,)),
            pltpu.SemaphoreType.DMA((COPIES,)), pltpu.SemaphoreType.DMA((COPIES,)),
        ],
        compiler_params=pltpu.CompilerParams(
            collective_id=0, has_side_effects=True, vmem_limit_bytes=60 * 2**20),
    )(momentum, gradient, basis)


def close_kernel(low, basis, mom, grad, mom_out, update_out, basis_out):
    n = mom.shape[0]
    products = lax.dot_general(low[...], basis[...], (((1,), (1,)), ((), ())), preferred_element_type=F32)
    mom_out[...] = mom[...] + grad[...].astype(F32) - (1.0 - DECAY) * products[:n]
    update_out[...] = (math.sqrt(ROWS_FF / RANK) * products[n:]).astype(BF16)
    basis_out[...] = basis[...]


def close(low, basis, momentum, gradient):
    n, columns = momentum.shape
    width = 7 * NB
    across = pl.BlockSpec((n, width), lambda j: (0, j))
    along = pl.BlockSpec((width, RANK), lambda j: (j, 0))
    return pl.pallas_call(
        close_kernel,
        grid=(columns // width,),
        in_specs=[pl.BlockSpec((2 * n, RANK), lambda j: (0, 0)), along, across, across],
        out_specs=(across, across, along),
        out_shape=(jax.ShapeDtypeStruct((n, columns), F32), jax.ShapeDtypeStruct((n, columns), BF16),
                   jax.ShapeDtypeStruct((columns, RANK), BF16)),
        compiler_params=pltpu.CompilerParams(vmem_limit_bytes=60 * 2**20),
    )(low, basis, momentum, gradient)


def body(momentum, gradient, column_basis):
    low, new_basis = dion(momentum, gradient, column_basis)
    return close(low, new_basis, momentum, gradient)


def solution(mesh):
    placed = (P("fsdp", "tp"), P("fsdp", "tp"), P("tp", None))
    return jax.shard_map(
        body,
        mesh=mesh,
        in_specs=placed,
        out_specs=(P("fsdp", "tp"), P("fsdp", "tp"), P("tp", None)),
        check_vma=False,
    )
```

```python
import math

import jax
import jax.numpy as jnp
from jax import lax
from jax.experimental import pallas as pl
from jax.experimental.pallas import tpu as pltpu
from jax.sharding import PartitionSpec as P

ROWS_FF = 18432
COLS_D = 7168
RANK = 896

RIDGE = 0.001
DECAY = 0.8
EPS = 1e-06
HI = lax.Precision.HIGHEST
F32 = jnp.float32
BF16 = jnp.bfloat16
NB = 128
NBLK = RANK // NB
MESH = pl.DeviceIdType.MESH
NX, NY, NZ = 4, 4, 8


class Links:
    def __init__(self):
        f = lax.axis_index("fsdp")
        self.x = lax.axis_index("tp")
        self.core = lax.rem(f, 2)
        self.z = lax.rem(f // 2, NZ)
        self.y = f // (2 * NZ)

    def at_x(self, d):
        t = lax.rem(self.x + d, NX)
        return t, {"tp": t}

    def at_y(self, d):
        t = lax.rem(self.y + d, NY)
        return t, {"fsdp": (t * NZ + self.z) * 2 + self.core}

    def at_z(self, d):
        t = lax.rem(self.z + d, NZ)
        return t, {"fsdp": (self.y * NZ + t) * 2 + self.core}

    def at_zc(self, d):
        t = lax.rem(self.z * 2 + self.core + d, 2 * NZ)
        return t, {"fsdp": self.y * NZ * 2 + t}

    def at_xy(self, dx, dy):
        tx, ty = lax.rem(self.x + dx, NX), lax.rem(self.y + dy, NY)
        return tx * NY + ty, {"tp": tx, "fsdp": (ty * NZ + self.z) * 2 + self.core}

    def at_core(self):
        t = 1 - self.core
        return t, {"fsdp": (self.y * NZ + self.z) * 2 + t}


class Copies:
    def __init__(self, send_sems, recv_sems):
        self.send_sems, self.recv_sems = send_sems, recv_sems
        self.count = 0
        self.started = []

    def make(self, src, dst, device, when=None, slot=None):
        arrival = self.count if slot is None else slot
        copy = pltpu.make_async_remote_copy(
            src_ref=src, dst_ref=dst, send_sem=self.send_sems.at[self.count],
            recv_sem=self.recv_sems.at[arrival], device_id=device, device_id_type=MESH)
        self.count += 1
        self.started.append((copy, when))
        return copy

    def start(self, src, dst, device, when=None, slot=None):
        copy = self.make(src, dst, device, when, slot)
        if when is None:
            copy.start()
        else:
            pl.when(when)(copy.start)
        return copy

    def finish(self):
        for copy, when in self.started:
            if when is None:
                copy.wait_send()
            else:
                pl.when(when)(copy.wait_send)
        self.started = []


def greet(links, along):
    barrier = pltpu.get_barrier_semaphore()
    partners = []
    if "x" in along:
        partners += [links.at_x(d)[1] for d in range(1, NX)]
    if "y" in along:
        partners += [links.at_y(d)[1] for d in range(1, NY)]
    if "z" in along:
        partners += [links.at_z(d)[1] for d in range(1, NZ)]
    if "c" in along:
        partners += [links.at_core()[1]]
    if "Z" in along:
        partners += [links.at_zc(d)[1] for d in range(1, 2 * NZ)]
    if "X" in along:
        partners += [links.at_xy(dx, dy)[1] for dx in range(NX) for dy in range(NY) if dx or dy]
    for device in partners:
        pl.semaphore_signal(barrier, inc=1, device_id=device, device_id_type=MESH)
    return barrier, len(partners)


def rows(start, size):
    return pl.ds(pl.multiple_of(start, 8), size)


def cross_part(low, projected, half, part):
    lhs = low[:, pl.ds(pl.multiple_of(half * RANK + part.start, NB), part.size)]
    p = projected[...]
    high = p.astype(BF16)
    rest = (p - high.astype(F32)).astype(BF16)
    dims = (((0,), (0,)), ((), ()))
    return (lax.dot_general(lhs, high, dims, preferred_element_type=F32)
            + lax.dot_general(lhs, rest, dims, preferred_element_type=F32))


def factor128(tiles):
    lane = lax.broadcasted_iota(jnp.int32, (8, 128), 1)
    sub = lax.broadcasted_iota(jnp.int32, (8, 128), 0)
    tiles = list(tiles)
    out = []

    def over_lanes(x, c):
        return jnp.broadcast_to(x[:, c:c + 1], (8, 128))

    def over_rows(x, r):
        return jnp.broadcast_to(x[r:r + 1, :], (8, 128))

    diag = [over_lanes(tiles[0], c) for c in range(8)]
    for s in range(16):
        a = {(r, c): over_rows(diag[c], r) for c in range(8) for r in range(c, 8)}
        inside = (lane >= 8 * s) & (lane < 8 * s + 8)
        row = jnp.where(inside, jnp.where(lane - 8 * s == sub, 1.0, 0.0), tiles[s])
        y = [over_rows(row, r) for r in range(8)]
        inv, low = [None] * 8, {}
        for j in range(8):
            inv[j] = pl.reciprocal(a[j, j], approx=False)
            for i in range(j + 1, 8):
                low[i, j] = a[i, j] * inv[j]
            for i in range(j + 1, 8):
                for k in range(j + 1, i + 1):
                    a[i, k] = a[i, k] - low[i, j] * a[k, j]
            for i in range(j + 1, 8):
                y[i] = y[i] - low[i, j] * y[j]
        z = [y[j] * inv[j] for j in range(8)]
        done = y[0] * lax.rsqrt(a[0, 0])
        for j in range(1, 8):
            done = jnp.where(sub == j, y[j] * lax.rsqrt(a[j, j]), done)
        out.append(jnp.where(lane < 8 * s + 8, done, 0.0))
        if s == 15:
            break
        q = [None] * 8
        for j in range(7, -1, -1):
            q[j] = z[j]
            for i in range(j + 1, 8):
                q[j] = q[j] - low[i, j] * q[i]
        for t in range(s + 1, 16):
            col = [over_lanes(tiles[t], 8 * s + c) for c in range(8)]
            acc = jnp.where(inside, 0.0, tiles[t])
            if t == s + 1:
                for j in range(8):
                    for i in range(j + 1, 8):
                        col[i] = col[i] - low[i, j] * col[j]
                for j in range(8):
                    acc = acc - col[j] * z[j]
                diag = [over_lanes(tiles[t], 8 * t + c) for c in range(8)]
                for j in range(8):
                    scaled = col[j] * inv[j]
                    for c in range(8):
                        diag[c] = diag[c] - col[j] * over_rows(scaled, c)
            else:
                for j in range(8):
                    acc = acc - col[j] * q[j]
            tiles[t] = acc
    return out


def assemble(g_ref, w):
    eye = jnp.where(
        lax.broadcasted_iota(jnp.int32, (NB, NB), 0) == lax.broadcasted_iota(jnp.int32, (NB, NB), 1), RIDGE, 0.0)
    for d in range(4):
        for b in range(NBLK):
            c = (b + d) % NBLK
            block = g_ref[d // 2, d % 2, b * NB:(b + 1) * NB, :]
            if d == 0:
                block = block + eye
            if b <= c:
                w[b * NB:(b + 1) * NB, c * NB:(c + 1) * NB] = block
            else:
                w[c * NB:(c + 1) * NB, b * NB:(b + 1) * NB] = block.T


def two(x):
    high = x.astype(BF16)
    return high, (x - high.astype(F32)).astype(BF16)


def times_inverse(left, w, k):
    n = (k + 1) * NB
    high, low = two(left[:, :n])
    w_high, w_low = two(w[k * NB:n, :n])
    return lax.dot_general(
        jnp.concatenate([high, high, low], axis=1), jnp.concatenate([w_high, w_low, w_high], axis=1),
        (((1,), (1,)), ((), ())), preferred_element_type=F32)


def block(i):
    return slice(i * NB, (i + 1) * NB)


def dot_rows(a, b):
    return lax.dot_general(a, b, (((0,), (0,)), ((), ())), precision=HI, preferred_element_type=F32)


def split(x):
    high = x.astype(BF16)
    rest = x - high.astype(F32)
    mid = rest.astype(BF16)
    return high, mid, (rest - mid.astype(F32)).astype(BF16)


def terms(x):
    high, mid, low = split(x)
    return (high, mid, high, low, high, mid), (high, high, mid, high, low, mid)


def factor(w, lefts, rights, amid, beside):
    w[pl.ds(RANK, NB), :] = jnp.zeros((NB, RANK), F32)
    lefts[:, pl.ds(RANK, NB)] = jnp.zeros((6 * NB, NB), BF16)

    def step(k, _):
        o = pl.multiple_of(k * NB, NB)
        at = pl.ds(o, NB)
        inv = jnp.concatenate(
            factor128([w[pl.ds(pl.multiple_of(o + 8 * t, 8), 8), at] for t in range(16)]), axis=0)
        for when, act in amid.items():
            pl.when(k == when)(act)
        left = jnp.concatenate(terms(inv)[0], axis=1)
        right = jnp.concatenate(terms(w[at, :])[1], axis=0)
        w[at, :] = jnp.dot(left, right, preferred_element_type=F32)
        w[at, at] = inv
        left, right = terms(w[at, :])
        for i in range(6):
            lefts[block(i), pl.ds(0, RANK)] = left[i]
            rights[block(i), :] = right[i]

        def update(i, _):
            below = pl.ds(pl.multiple_of((k + 1 + 2 * i) * NB, NB), 2 * NB)
            w[below, at] = jnp.zeros((2 * NB, NB), F32)
            w[below, :] -= lax.dot_general(
                lefts[:, below], rights[...], (((0,), (0,)), ((), ())), preferred_element_type=F32)
            return 0

        lax.fori_loop(0, (NBLK - k) // 2, update, 0)
        for when, act in beside.items():
            pl.when(k == when)(act)
        return 0

    lax.fori_loop(0, NBLK, step, 0)


OWN = 7
COPIES = 3 + 1 + 6 + 6 + 5 + 3 + 6 + 6 + 8 + 1 + 3 + 7 + 7 + 3 + 15 + 15 + 7 + 3 + 3 + 7 + 2 + 7 + 1


def step_kernel(mom_any, grad_any, basis_any, low_any, nb_any, pp, prx, pc, pf, ga, r1, s1, r2, zin, zp, zr, zt, a4, gf, low,
                so, sr, s, w, ra1, sa, ra2, ring_up, ring_down, acc_up, acc_down, sb, rb2, sq1, sq2, nb, xf,
                lefts, rights, mom, grad, basis, low_out, nb_out, in_sem, out_sem, ssem, rsem):
    inputs = [pltpu.make_async_copy(src, dst, in_sem.at[i])
              for i, (src, dst) in enumerate(((mom_any, mom), (grad_any, grad), (basis_any, basis)))]
    for copy in inputs:
        copy.start()
    lk = Links()
    cp = Copies(ssem, rsem)
    barrier, partners = greet(lk, "ZX")
    n = pp.shape[0]
    part = n // NX
    core_dev = lk.at_core()[1]

    def project(h):
        at = pl.ds(pl.multiple_of(h * (n // 2), 16), n // 2)
        low[at, :] = (mom[at, :] + grad[at, :].astype(F32)).astype(BF16)
        pp[at, :] = jnp.dot(low[at, :], basis[...], preferred_element_type=F32)

    for copy in inputs:
        copy.wait()
    mine_half = lk.x // 2
    project(1 - mine_half)
    pl.semaphore_wait(barrier, partners)
    sent = []
    for i in range(2):
        t = (1 - mine_half) * 2 + i
        slot = lax.rem(t - lk.x + NX, NX) - 1
        sent.append(cp.start(pp.at[rows(t * part, part)], prx.at[slot], {"tp": t}, slot=slot))
    project(mine_half)
    t = mine_half * 2 + 1 - lax.rem(lk.x, 2)
    slot = lax.rem(t - lk.x + NX, NX) - 1
    sent.append(cp.start(pp.at[rows(t * part, part)], prx.at[slot], {"tp": t}, slot=slot))
    for copy in sent:
        copy.wait_recv()
    mine = pp[rows(lk.x * part, part), :] + prx[0] + prx[1] + prx[2]
    pf[rows(lk.x * part, part), :] = mine
    pc[rows(lk.core * part, part), pl.ds(0, RANK)] = mine
    own = pc.at[rows(lk.core * part, part), pl.ds(0, RANK)]
    copy = cp.start(own, own, core_dev)
    copy.wait_recv()
    pc[:, pl.ds(RANK, 3 * NB)] = pc[:, pl.ds(0, 3 * NB)]

    for b in range(NBLK):
        blocks = dot_rows(pc[:, pl.ds(b * NB, NB)],
                          pc[:, pl.ds(pl.multiple_of((b + 2 * lk.core) * NB, NB), 2 * NB)])
        ga[0, pl.ds(b * NB, NB), :] = blocks[:, :NB]
        ga[1, pl.ds(b * NB, NB), :] = blocks[:, NB:]

    big, small = RANK // 4, RANK // 16
    sent = []
    for d in range(1, 4):
        tx, dx = lk.at_x(d)
        ty, dy = lk.at_y(d)
        sent.append(cp.start(ga.at[0, rows(tx * big, big)], r1.at[0, d - 1], dx))
        sent.append(cp.start(ga.at[1, rows(ty * big, big)], r1.at[1, d - 1], dy))
    for copy in sent:
        copy.wait_recv()
    s1[0] = ga[0, rows(lk.x * big, big), :] + r1[0, 0] + r1[0, 1] + r1[0, 2]
    s1[1] = ga[1, rows(lk.y * big, big), :] + r1[1, 0] + r1[1, 1] + r1[1, 2]
    sent = []
    for d in range(1, 4):
        tx, dx = lk.at_x(d)
        ty, dy = lk.at_y(d)
        sent.append(cp.start(s1.at[0, rows(ty * small, small)], r2.at[0, d - 1], dy))
        sent.append(cp.start(s1.at[1, rows(tx * small, small)], r2.at[1, d - 1], dx))
    rest = []
    own = pf.at[rows(lk.x * part, part)]
    for d in range(1, NX):
        rest.append(cp.start(own, own, lk.at_x(d)[1]))
    for copy in sent:
        copy.wait_recv()
    zin[0] = s1[0, rows(lk.y * small, small), :] + r2[0, 0] + r2[0, 1] + r2[0, 2]
    zin[1] = s1[1, rows(lk.x * small, small), :] + r2[1, 0] + r2[1, 1] + r2[1, 2]
    even = lax.rem(lk.z, 2)
    pair = lk.at_z(NZ + 1 - 2 * even)[1]
    copy = cp.start(zin.at[1 - even], zp, pair)
    copy.wait_recv()
    zr[lk.z // 2] = zin[even] + zp[...]
    sent = [cp.start(zr.at[lk.z // 2], zr.at[lk.z // 2], lk.at_z(d)[1]) for d in (2, 4, 6)]
    for copy in sent:
        copy.wait_recv()
    zt[even] = zr[0] + zr[1] + zr[2] + zr[3]
    copy = cp.start(zt.at[even], zt.at[even], pair)
    copy.wait_recv()

    a4[0, rows(lk.y * small, small), :] = zt[0]
    a4[1, rows(lk.x * small, small), :] = zt[1]
    sent = []
    for d in range(1, 4):
        own0 = a4.at[0, rows(lk.y * small, small)]
        own1 = a4.at[1, rows(lk.x * small, small)]
        sent.append(cp.start(own0, own0, lk.at_y(d)[1]))
        sent.append(cp.start(own1, own1, lk.at_x(d)[1]))
    for copy in sent:
        copy.wait_recv()
    gf[lk.core, 0, rows(lk.x * big, big), :] = a4[0]
    gf[lk.core, 1, rows(lk.y * big, big), :] = a4[1]
    own0 = gf.at[lk.core, 0, rows(lk.x * big, big)]
    own1 = gf.at[lk.core, 1, rows(lk.y * big, big)]
    sent = []
    for d in range(1, 4):
        sent.append((cp.start(own0, own0, lk.at_x(d)[1]), 0, lax.rem(lk.x + 4 - d, 4)))
        sent.append((cp.start(own1, own1, lk.at_y(d)[1]), 1, lax.rem(lk.y + 4 - d, 4)))
    across = [cp.start(own0, own0, core_dev), cp.start(own1, own1, core_dev)]
    for copy in rest:
        copy.wait_recv()
    parts = (pl.ds(3 * NB, 4 * NB), pl.ds(0, 3 * NB))
    cross = []
    for at in parts:
        so[at, :] = cross_part(low, pf, 1 - lk.core, at)
        cross.append(cp.start(so.at[at], sr.at[at], core_dev))
    for at in parts:
        s[at, :] = cross_part(low, pf, lk.core, at)
    for copy, h, t in sent:
        copy.wait_recv()
        piece = gf.at[lk.core, h, rows(t * big, big)]
        across.append(cp.start(piece, piece, core_dev))

    half = RANK // 2
    ya, za, piece = half // NY, half // OWN, half // NY // OWN
    owner = lk.z < OWN
    zc = jnp.minimum(lk.z, OWN - 1)

    def ring_rows(shift):
        return rows(half + jnp.minimum(lax.rem(lk.z + NZ + shift, NZ), OWN - 1) * za, za)

    up, down = lk.at_z(1)[1], lk.at_z(NZ - 1)[1]
    ups = [cp.make(s.at[ring_rows(4)] if i == 0 else acc_up.at[i - 1], ring_up.at[i], up) for i in range(4)]
    downs = [cp.make(s.at[ring_rows(-3)] if i == 0 else acc_down.at[i - 1], ring_down.at[i], down) for i in range(3)]
    first_a = []
    for d in range(1, NY):
        t, dev = lk.at_y(d)
        first_a.append(cp.make(s.at[rows(t * ya, ya)], ra1.at[d - 1], dev))
    second_a = []
    for d in range(1, NZ):
        t, dev = lk.at_z(d)
        src = sa.at[rows(jnp.minimum(t, OWN - 1) * piece, piece)]
        second_a.append(cp.make(src, ra2.at[d - 1], dev))
    ring_at = {shift: ring_rows(shift) for shift in (3, 2, 1, -2, -1)}
    own_ya = rows(lk.y * ya, ya)

    def ring_step(i):
        ups[i - 1].wait_recv()
        acc_up[i - 1] = s[ring_at[4 - i], :] + ring_up[i - 1]
        ups[i].start()
        if i < 3:
            downs[i - 1].wait_recv()
            acc_down[i - 1] = s[ring_at[i - 3], :] + ring_down[i - 1]
            downs[i].start()

    def turn_a():
        for copy in first_a:
            copy.wait_recv()
        sa[...] = s[own_ya, :] + ra1[0] + ra1[1] + ra1[2]
        for copy in second_a:
            copy.start()

    second_b = []
    for d in range(1, NY):
        t, dev = lk.at_y(d)
        second_b.append(cp.make(sb.at[rows(t * piece, piece)], rb2.at[d - 1], dev))
    own_za = rows(half + zc * za, za)

    def turn_b():
        ups[3].wait_recv()
        downs[2].wait_recv()
        sb[...] = s[own_za, :] + ring_up[3] + ring_down[2]
        for copy in second_b:
            copy.start()

    for at, copy, ready in zip(parts, cross, ([ups[0], downs[0]], first_a)):
        copy.wait_recv()
        s[at, :] += sr[at, :]
        for after in ready:
            after.start()
    for copy in across:
        copy.wait_recv()
    assemble(gf, w)
    factor(w, lefts, rights, {3: turn_a},
           {0: lambda: ring_step(1), 1: lambda: ring_step(2), 2: lambda: ring_step(3), 5: turn_b})
    for copy in second_b:
        copy.wait_recv()
    left_b = sb[rows(lk.y * piece, piece), :] + rb2[0] + rb2[1] + rb2[2]
    for copy in second_a:
        copy.wait_recv()
    left_a = sa[rows(zc * piece, piece), :]
    for i in range(NZ - 1):
        left_a = left_a + ra2[i]

    left = jnp.concatenate([left_a, left_b], axis=0)
    right = [times_inverse(left, w, k) for k in range(NBLK)]
    me1 = lk.z * 2 + lk.core
    me2 = lk.x * NY + lk.y
    base = lk.core * RANK
    at_a = rows16(base + lk.y * ya + zc * piece, piece)
    at_b = rows16(base + half + zc * za + lk.y * piece, piece)
    for k in range(NBLK):
        rounded = right[k].astype(BF16)

        @pl.when(owner)
        def _():
            nb[at_a, block(k)] = rounded[:piece]
            nb[at_b, block(k)] = rounded[piece:]

        sq1[me1, k:k + 1, :] = jnp.where(owner, jnp.sum(right[k] * right[k], axis=0, keepdims=True), 0.0)
    sq1[me1, NBLK:, :] = jnp.zeros((1, NB), F32)
    own = nb.at[at_b]
    gather_b = [cp.start(own, own, lk.at_y(d)[1], when=owner) for d in range(1, NY)]
    own = nb.at[at_a]
    gather_a = [cp.start(own, own, lk.at_z(d)[1], when=owner) for d in range(1, NZ)]
    squares = [cp.start(sq1.at[me1], sq1.at[me1], lk.at_zc(d)[1]) for d in range(1, 2 * NZ)]

    def owned(shift):
        return lax.rem(lk.z + NZ + shift, NZ) < OWN

    def part_b(shift):
        return nb.at[rows16(base + half + jnp.minimum(lax.rem(lk.z + NZ + shift, NZ), OWN - 1) * za, za)]

    @pl.when(owner)
    def _():
        for copy in gather_b:
            copy.wait_recv()

    ups = [cp.start(part_b(0), part_b(0), up, when=owned(0))]
    downs = [cp.start(part_b(0), part_b(0), down, when=owned(0))]
    passed = []

    def pass_on(shift):
        piece_b = part_b(shift)
        passed.append((cp.start(piece_b, piece_b, core_dev, when=owned(shift)), owned(shift)))

    pass_on(0)

    def gather_step(i):
        pl.when(owned(-i))(ups[-1].wait_recv)
        ups.append(cp.start(part_b(-i), part_b(-i), up, when=owned(-i)))
        pass_on(-i)
        if i < 3:
            pl.when(owned(i))(downs[-1].wait_recv)
            downs.append(cp.start(part_b(i), part_b(i), down, when=owned(i)))
            pass_on(i)

    def ortho(first, last):
        for k in range(first, last):
            xf[:, block(k)] = times_inverse(pf[...], w, k)

    ortho(0, 4)
    gather_step(1)
    for d in range(1, NZ):
        pl.when(owned(-d))(gather_a[d - 1].wait_recv)
    own = nb.at[rows16(base + lk.y * ya, ya)]
    gather_a = [cp.start(own, own, lk.at_y(d)[1]) for d in range(1, NY)]
    for copy in squares:
        copy.wait_recv()
    total = sq1[0]
    for i in range(1, 2 * NZ):
        total = total + sq1[i]
    sq2[me2] = total
    squares = [cp.start(sq2.at[me2], sq2.at[me2], lk.at_xy(dx, dy)[1])
               for dx in range(NX) for dy in range(NY) if dx or dy]
    ortho(4, 6)
    gather_step(2)
    ortho(6, NBLK)
    gather_step(3)
    for copy in squares:
        copy.wait_recv()
    total = sq2[0]
    for i in range(1, NX * NY):
        total = total + sq2[i]
    rms = jnp.sqrt(total / COLS_D + EPS)
    for k in range(NBLK):
        low_out[:n, block(k)] = (xf[:, block(k)] * rms[k:k + 1, :]).astype(BF16)
        low_out[n:, block(k)] = xf[:, block(k)].astype(BF16)
    stores = [pltpu.make_async_copy(low_out, low_any, out_sem.at[4])]
    stores[0].start()
    for copy in gather_a:
        copy.wait_recv()
    own = nb.at[rows16(base, half)]
    across = [cp.start(own, own, core_dev)]
    scale = 1.0 / rms

    def normalize(start, size):
        at = rows16(start, size)
        for k in range(NBLK):
            nb_out[at, block(k)] = (nb[at, block(k)].astype(F32) * scale[k:k + 1, :]).astype(BF16)
        stores.append(pltpu.make_async_copy(nb_out.at[at], nb_any.at[at], out_sem.at[len(stores) - 1]))
        stores[-1].start()

    normalize(base, half)
    pl.when(owned(-4))(ups[-1].wait_recv)
    pl.when(owned(3))(downs[-1].wait_recv)
    pass_on(-4)
    pass_on(3)
    normalize(base + half, half)
    across[0].wait_recv()
    normalize((1 - lk.core) * RANK, half)
    for copy, arrives in passed:
        pl.when(arrives)(copy.wait_recv)
    normalize((1 - lk.core) * RANK + half, half)
    for copy in stores:
        copy.wait()
    cp.finish()


def rows16(start, size):
    return pl.ds(pl.multiple_of(start, 16), size)


def dion(momentum, gradient, basis):
    n, columns = momentum.shape
    half, big, small = RANK // 2, RANK // 4, RANK // 16
    ya, za, piece = half // NY, half // OWN, half // NY // OWN

    def buffer(*shape, dtype=F32):
        return pltpu.VMEM(shape, dtype)

    return pl.pallas_call(
        step_kernel,
        out_shape=(jax.ShapeDtypeStruct((2 * n, RANK), BF16), jax.ShapeDtypeStruct((columns, RANK), BF16)),
        in_specs=[pl.BlockSpec(memory_space=pl.ANY)] * 3,
        out_specs=(pl.BlockSpec(memory_space=pl.ANY),) * 2,
        scratch_shapes=[
            buffer(n, RANK), buffer(3, n // NX, RANK), buffer(2 * n // NX, RANK + 3 * NB), buffer(n, RANK),
            buffer(2, RANK, NB), buffer(2, 3, big, NB), buffer(2, big, NB), buffer(2, 3, small, NB),
            buffer(2, small, NB), buffer(small, NB), buffer(4, small, NB), buffer(2, small, NB),
            buffer(2, big, NB), buffer(2, 2, RANK, NB), buffer(n, columns, dtype=BF16),
            buffer(RANK, RANK), buffer(RANK, RANK), buffer(RANK, RANK), buffer(RANK + NB, RANK),
            buffer(NY - 1, ya, RANK), buffer(ya, RANK), buffer(NZ - 1, piece, RANK),
            buffer(4, za, RANK), buffer(3, za, RANK), buffer(3, za, RANK), buffer(2, za, RANK),
            buffer(za, RANK), buffer(NY - 1, piece, RANK),
            buffer(2 * NZ, 8, NB), buffer(NX * NY, 8, NB), buffer(columns, RANK, dtype=BF16),
            buffer(n, RANK),
            buffer(6 * NB, RANK + NB, dtype=BF16), buffer(6 * NB, RANK, dtype=BF16),
            buffer(n, columns), buffer(n, columns, dtype=BF16), buffer(columns, RANK, dtype=BF16),
            buffer(2 * n, RANK, dtype=BF16), buffer(columns, RANK, dtype=BF16),
            pltpu.SemaphoreType.DMA((3,)), pltpu.SemaphoreType.DMA((5,)),
            pltpu.SemaphoreType.DMA((COPIES,)), pltpu.SemaphoreType.DMA((COPIES,)),
        ],
        compiler_params=pltpu.CompilerParams(
            collective_id=0, has_side_effects=True, vmem_limit_bytes=60 * 2**20),
    )(momentum, gradient, basis)


def close_kernel(low, basis, mom, grad, mom_out, update_out, basis_out):
    n = mom.shape[0]
    products = lax.dot_general(low[...], basis[...], (((1,), (1,)), ((), ())), preferred_element_type=F32)
    mom_out[...] = mom[...] + grad[...].astype(F32) - (1.0 - DECAY) * products[:n]
    update_out[...] = (math.sqrt(ROWS_FF / RANK) * products[n:]).astype(BF16)
    basis_out[...] = basis[...]


def close(low, basis, momentum, gradient):
    n, columns = momentum.shape
    width = 7 * NB
    across = pl.BlockSpec((n, width), lambda j: (0, j))
    along = pl.BlockSpec((width, RANK), lambda j: (j, 0))
    return pl.pallas_call(
        close_kernel,
        grid=(columns // width,),
        in_specs=[pl.BlockSpec((2 * n, RANK), lambda j: (0, 0)), along, across, across],
        out_specs=(across, across, along),
        out_shape=(jax.ShapeDtypeStruct((n, columns), F32), jax.ShapeDtypeStruct((n, columns), BF16),
                   jax.ShapeDtypeStruct((columns, RANK), BF16)),
        compiler_params=pltpu.CompilerParams(vmem_limit_bytes=60 * 2**20),
    )(low, basis, momentum, gradient)


def body(momentum, gradient, column_basis):
    low, new_basis = dion(momentum, gradient, column_basis)
    return close(low, new_basis, momentum, gradient)


def solution(mesh):
    placed = (P("fsdp", "tp"), P("fsdp", "tp"), P("tp", None))
    return jax.shard_map(
        body,
        mesh=mesh,
        in_specs=placed,
        out_specs=(P("fsdp", "tp"), P("fsdp", "tp"), P("tp", None)),
        check_vma=False,
    )
```
